256 devices in a mesh: dp: 16 (over x_lo, y, core), tensor: 16 (over z, x_hi).
Axes of the slice: x: 4 (x_hi: 2, x_lo: 2; x = x_hi * 2 + x_lo), y: 4, z: 8, core: 2. Of those that a mesh axis runs over, the one named last changes fastest.
Arguments:
- tokens: bfloat16 [8192, 4096], P(('dp', 'tensor')), may hold values from -24 to 24
- cotangent: bfloat16 [8192, 4096], P(('dp', 'tensor')), may hold values from -24 to 24
- w_in: bfloat16 [4096, 8192], P(None, 'tensor'), may hold values from -0.09375 to 0.09375
- w_out: bfloat16 [8192, 4096], P('tensor'), may hold values from -0.0625 to 0.0625
Outputs:
- grad_tokens: bfloat16 [8192, 4096], P(('dp', 'tensor'))
- grad_in: bfloat16 [4096, 8192], P('dp', 'tensor')
- grad_out: bfloat16 [8192, 4096], P('tensor', 'dp')
The draws below stay inside these ranges and needn't reach their ends.
All inputs are finite; a program needn't handle non-finite values.
Results may differ from the reference program's by a relative error of at most 0.023.
Values may be sent and summed in bfloat16 or wider, within the bound.
A program may use at most 128 MiB of HBM per device.

```python
import jax
import jax.numpy as jnp
from jax import lax

D = 4096
FF = 8192
TOK_GRP = 512
TOKENS = 8192
N_DP = 16
N_TENSOR = 16


def with_spikes(entries, rng, source, target, blocks, factor):
    owner, partner = [(jnp.arange(entries.shape[dim]) // (entries.shape[dim] // blocks)).reshape([-1 if axis == dim else 1 for axis in range(entries.ndim)]) for dim in (source, target)]
    chosen = jax.random.permutation(rng, blocks)[partner]
    strong = (owner == chosen) | (owner == (partner + blocks // 2) % blocks)
    return jnp.where(strong, factor * entries, entries)


def block_scale(rng, dims, split, low, high):
    def one(axis_at, shards_of):
        draws = jax.random.uniform(jax.random.fold_in(jax.random.fold_in(rng, 6), axis_at), (shards_of,), jnp.float32, low / len(split), high / len(split))
        return jnp.repeat(jnp.exp(draws), dims[axis_at] // shards_of).reshape((-1,) + (1,) * (len(dims) - axis_at - 1))

    gain = one(*split[0])
    for cut in split[1:]:
        gain = gain * one(*cut)
    return gain


def gaussian(rng, shape, deviation, bound, pieces=(), kind=jnp.bfloat16):
    result = deviation * jax.random.normal(rng, shape, jnp.float32)
    if pieces:
        result = result * block_scale(rng, shape, pieces, -0.22, 0.18)
    return jnp.clip(result, -bound, bound).astype(kind)


def noise_with(key, shape, scale, bound, pieces, heavy, dtype=jnp.bfloat16):
    drawn = scale * jax.random.normal(key, shape, jnp.float32)
    if pieces:
        drawn = drawn * block_scale(key, shape, pieces, -0.22, 0.18)
    return jnp.clip(with_spikes(drawn, jax.random.fold_in(key, 3), *heavy), -bound, bound).astype(dtype)


def setup_inputs(seed: int = 0) -> dict:
    arg_keys = jax.random.split(jax.random.key(seed), 5)
    return {
        "tokens": noise_with(arg_keys[0], (TOKENS, D), 1.0, 24.0, ((0, 256),), (0, 1, 256, 6.0)),
        "cotangent": noise_with(arg_keys[1], (TOKENS, D), 1.0, 24.0, ((0, 256),), (0, 1, 256, 6.0)),
        "w_in": gaussian(arg_keys[2], (D, FF), D ** -0.5, 0.09375, ((1, 16),)),
        "w_out": gaussian(arg_keys[3], (FF, D), FF ** -0.5, 0.0625, ((0, 16),)),
    }


cubic_coef = 0.044715
root_coef = 0.7978845608028654

def gelu_parts(pre):
    inner = root_coef * (pre + cubic_coef * pre * pre * pre)
    tangent = jnp.tanh(inner)
    value = 0.5 * pre * (1.0 + tangent)
    slope = 0.5 * (1.0 + tangent) + 0.5 * pre * (1.0 - tangent * tangent) * root_coef * (1.0 + 3.0 * cubic_coef * pre * pre)
    return (value, slope)

def rounded(value):
    return lax.optimization_barrier(value.astype(jnp.bfloat16)).astype(jnp.float32)

def reference(tokens, cotangent, w_in, w_out):
    scale_factor = 1.0 / jnp.sqrt(jnp.float32(TOKENS))
    group_tokens = tokens.reshape(N_DP, TOK_GRP, D)
    group_cots = cotangent.reshape(N_DP, TOK_GRP, D)
    block_cols = FF // N_TENSOR
    w_blocks = w_in.reshape(D, N_TENSOR, block_cols).astype(jnp.float32)

    def step(totals, inputs):
        group_x, group_dy = inputs
        pre = jnp.dot(group_x, w_in, preferred_element_type=jnp.float32)
        value, slope = gelu_parts(pre)
        act = value.astype(jnp.bfloat16)
        dact = lax.dot_general(group_dy, w_out, (((1,), (1,)), ((), ())), preferred_element_type=jnp.float32)
        dpre = (dact * slope).astype(jnp.bfloat16)
        dpre_blocks = dpre.reshape(TOK_GRP, N_TENSOR, block_cols).astype(jnp.float32)
        partials = jnp.einsum('gkf,dkf->kgd', dpre_blocks, w_blocks)
        grad_x = lax.optimization_barrier(jnp.sum(rounded(partials), axis=0)).astype(jnp.bfloat16)
        part_in = lax.dot_general(group_x, dpre, (((0,), (0,)), ((), ())), preferred_element_type=jnp.float32) * scale_factor
        part_out = lax.dot_general(act, group_dy, (((0,), (0,)), ((), ())), preferred_element_type=jnp.float32) * scale_factor
        return ((totals[0] + rounded(part_in), totals[1] + rounded(part_out)), grad_x)
    start_totals = (jnp.zeros((D, FF), jnp.float32), jnp.zeros((FF, D), jnp.float32))
    totals, grad_rows = lax.scan(step, start_totals, (group_tokens, group_cots))
    grad_tokens = grad_rows.reshape(TOKENS, D)
    return (grad_tokens, totals[0].astype(jnp.bfloat16), totals[1].astype(jnp.bfloat16))
```

```python
import functools
import math

import jax
import jax.numpy as jnp
from jax import lax
from jax.experimental import pallas as pl
from jax.experimental.pallas import tpu as pltpu
from jax.sharding import PartitionSpec as P

MESH = pl.DeviceIdType.MESH
F32, BF16 = jnp.float32, jnp.bfloat16
CUBIC, ROOT = 0.044715, 0.7978845608028654

SHARD = 32
HALF = SHARD // 2
CHUNK = 4 * SHARD
Z, Y = 8, 4
OWN, PAIR = 0, 1
BELOW, ABOVE = 0, 1


def gelu_parts(pre):
    tangent = jnp.tanh(ROOT * (pre + CUBIC * pre * pre * pre))
    value = 0.5 * pre * (1.0 + tangent)
    slope = 0.5 * (1.0 + tangent) + 0.5 * pre * (1.0 - tangent * tangent) * ROOT * (
        1.0 + 3.0 * CUBIC * pre * pre
    )
    return value, slope


def row_of(side, way, hop):
    if hop == 0:
        return 3 * CHUNK + side * SHARD
    if hop == 4:
        return 3 * CHUNK + (2 + side) * SHARD
    return (hop - 1) * CHUNK + (2 * way + side) * SHARD


def nt(a, b):
    return lax.dot_general(a, b, (((1,), (1,)), ((), ())), preferred_element_type=F32)


class Links:
    def __init__(self, send_sems, recv_sems):
        self.send_sems, self.recv_sems = send_sems, recv_sems
        self.copies = {}

    def send(self, key, src, dst, device):
        at = len(self.copies)
        copy = pltpu.make_async_remote_copy(
            src_ref=src,
            dst_ref=dst,
            send_sem=self.send_sems.at[at],
            recv_sem=self.recv_sems.at[at],
            device_id=device,
            device_id_type=MESH,
        )
        copy.start()
        self.copies[key] = copy

    def arrived(self, key):
        self.copies[key].wait_recv()

    def finish(self):
        for copy in self.copies.values():
            copy.wait_send()


MESSAGES = 120


def kernel(
    tokens_ref, cotangent_ref, w_in_ref, w_out_ref,
    gtok_ref, gin_ref, gout_ref,
    tok, cot, win, wout, dpre, actt, dpret, gx,
    from_z, from_pair, from_pair_end,
    core_out, core_in, part_in, part_out, xl_in, xl_out, half_in, full_in,
    local_sems, send_sems, recv_sems,
):
    width, hidden = w_in_ref.shape
    block = width // 16
    dp, tensor = lax.axis_index("dp"), lax.axis_index("tensor")
    xlo, y, core = dp // (2 * Y), (dp // 2) % Y, dp % 2
    z, xhi = tensor // 2, tensor % 2

    def device(xlo, y, core, z, xhi):
        return (xlo * (2 * Y) + y * 2 + core, z * 2 + xhi)

    up = device(xlo, y, core, (z + 1) % Z, xhi)
    down = device(xlo, y, core, (z + Z - 1) % Z, xhi)
    pair = device(1 - xlo, y, core, z, 1 - xhi)
    twin = device(1 - xlo, y, core, z, xhi)
    north = device(xlo, (y + 1) % Y, core, z, xhi)
    south = device(xlo, (y + Y - 1) % Y, core, z, xhi)
    sibling = device(xlo, y, 1 - core, z, xhi)
    everyone = (up, down, pair, twin, north, south, sibling)

    loads = [
        pltpu.make_async_copy(src, dst, local_sems.at[i])
        for i, (src, dst) in enumerate(
            (
                (tokens_ref, tok.at[pl.ds(row_of(OWN, 0, 0), SHARD)]),
                (cotangent_ref, cot.at[pl.ds(row_of(OWN, 0, 0), SHARD)]),
                (w_in_ref, win),
                (w_out_ref, wout),
            )
        )
    ]
    for load in loads:
        load.start()

    barrier = pltpu.get_barrier_semaphore()
    for other in everyone:
        pl.semaphore_signal(barrier, inc=1, device_id=other, device_id_type=MESH)
    pl.semaphore_wait(barrier, len(everyone))

    links = Links(send_sems, recv_sems)
    onward = {BELOW: up, ABOVE: down}

    def slot(buf, side, way, hop, part=slice(0, SHARD)):
        return buf.at[pl.ds(row_of(side, way, hop) + part.start, part.stop - part.start)]

    def first_hop(name, src, buf, side):
        for way in (BELOW, ABOVE):
            links.send((name, side, way, 1), src, slot(buf, side, way, 1), onward[way])

    def relay(name, buf, side, way, hop):
        part = slice(0, SHARD)
        if hop == 3:
            part = slice(0, HALF) if way == BELOW else slice(HALF, SHARD)
        links.send(
            (name, side, way, hop + 1),
            slot(buf, side, way, hop, part),
            slot(buf, side, way, hop + 1, part),
            onward[way],
        )

    links.send(("x", PAIR, 0, 0), tokens_ref, slot(tok, PAIR, 0, 0), pair)
    first_hop("dy", cotangent_ref, cot, OWN)
    first_hop("x", tokens_ref, tok, OWN)
    links.send(("dy", PAIR, 0, 0), cotangent_ref, slot(cot, PAIR, 0, 0), pair)
    links.arrived(("x", PAIR, 0, 0))
    first_hop("x", slot(tok, PAIR, 0, 0), tok, PAIR)

    def forward(chunk):
        rows = pl.ds(chunk * CHUNK, CHUNK)
        for n in range(0, hidden, 256):
            cols = pl.ds(n, 256)
            pre = jnp.dot(tok[rows, :], win[:, cols], preferred_element_type=F32)
            dact = nt(cot[rows, :], wout[cols, :])
            value, slope = gelu_parts(pre)
            change = dact * slope
            dpre[rows, cols] = change.astype(BF16)
            actt[cols, rows] = value.T.astype(BF16)
            dpret[cols, rows] = change.T.astype(BF16)

        def columns(j, carry):
            at = pl.ds(pl.multiple_of(j * 512, 512), 512)
            gx[rows, at] = nt(dpre[rows, :], win[at, :]).astype(BF16)
            return carry

        lax.fori_loop(0, width // 512, columns, 0)

    mid = width // 2
    left, right = pl.ds(0, mid), pl.ds(mid, mid)

    def slot_id(way, hop):
        return 0 if hop == 0 else 7 if hop == 4 else 2 * hop - 1 + way

    def cross(way, hop):
        at = slot_id(way, hop)
        links.send(
            ("gx", PAIR, way, hop),
            gx.at[pl.ds(row_of(PAIR, way, hop), SHARD), right],
            from_pair.at[at],
            pair,
        )

    for hop in (1, 2, 3):
        for way in (BELOW, ABOVE):
            links.arrived(("dy", OWN, way, hop))
            relay("dy", cot, OWN, way, hop)
            links.send(
                ("dy", PAIR, way, hop),
                slot(cot, OWN, way, hop),
                slot(cot, PAIR, way, hop),
                pair,
            )
        for side in (OWN, PAIR):
            for way in (BELOW, ABOVE):
                links.arrived(("x", side, way, hop))
                relay("x", tok, side, way, hop)
        if hop == 1:
            for load in loads:
                load.wait()
            links.arrived(("dy", PAIR, 0, 0))
        else:
            for way in (BELOW, ABOVE):
                links.arrived(("dy", PAIR, way, hop - 1))
            forward(hop - 2)
    for way in (BELOW, ABOVE):
        part = slice(0, HALF) if way == BELOW else slice(HALF, SHARD)
        links.arrived(("dy", OWN, way, 4))
        links.send(
            ("dy", PAIR, way, 4),
            slot(cot, OWN, way, 4, part),
            slot(cot, PAIR, way, 4, part),
            pair,
        )
    for way in (BELOW, ABOVE):
        links.arrived(("dy", PAIR, way, 3))
    forward(2)
    for side in (OWN, PAIR):
        for way in (BELOW, ABOVE):
            links.arrived(("x", side, way, 4))
    for way in (BELOW, ABOVE):
        links.arrived(("dy", PAIR, way, 4))
    forward(3)

    back = {BELOW: down, ABOVE: up}
    pieces = ((OWN, left), (PAIR, left), (OWN, right))

    def add(dst, *others):
        total = dst[...].astype(F32)
        for other in others:
            total = total + other[...].astype(F32)
        dst[...] = total.astype(BF16)

    def hop_back(way, hop):
        if hop == 4:
            part = slice(0, HALF) if way == BELOW else slice(HALF, SHARD)
        else:
            part = slice(0, SHARD)
        for i, (side, cols) in enumerate(pieces):
            mine = gx.at[pl.ds(row_of(side, way, hop) + part.start, part.stop - part.start), cols]
            links.send(
                ("gz", i, way, hop),
                mine,
                from_z.at[i, way, hop - 1, pl.ds(part.start, part.stop - part.start)],
                back[way],
            )

    def take_in(way, hop):
        for i, (side, cols) in enumerate(pieces):
            part = slice(0, SHARD)
            if hop == 3:
                part = slice(0, HALF) if way == BELOW else slice(HALF, SHARD)
            links.arrived(("gz", i, way, hop + 1))
            rows = pl.ds(part.start, part.stop - part.start)
            add(
                gx.at[pl.ds(row_of(side, way, hop) + part.start, part.stop - part.start), cols],
                from_z.at[i, way, hop, rows],
            )

    def take_pair(way, hop):
        links.arrived(("gx", PAIR, way, hop))
        add(
            gx.at[pl.ds(row_of(OWN, way, hop), SHARD), right],
            from_pair.at[slot_id(way, hop)],
        )

    cross(0, 4)
    for hop in (3, 2, 1):
        for way in (BELOW, ABOVE):
            cross(way, hop)
    cross(0, 0)

    IN, OUT = 0, 1

    def product(array, dx, dy, dc):
        there = ((xlo + dx) % 2) * (2 * Y) + ((y + dy) % Y) * 2 + (core + dc) % 2
        cols = pl.ds(pl.multiple_of(there * block, block), block)
        lhs, rhs = (dpret, tok) if array == IN else (actt, cot)
        return jnp.dot(lhs[...], rhs[:, cols], preferred_element_type=F32)

    def to_sibling(array, dx, dy):
        core_out[array, dx, dy] = product(array, dx, dy, 1).astype(BF16)
        links.send(
            ("core", array, dx, dy),
            core_out.at[array, dx, dy],
            core_in.at[array, dx, dy],
            sibling,
        )

    def chip_sum(array, dx, dy):
        mine = product(array, dx, dy, 0)
        links.arrived(("core", array, dx, dy))
        return mine + core_in[array, dx, dy].astype(F32)

    rank = {0: 0, 1: 1, 2: 2, 3: 3}
    mid_h = hidden // 2
    h_lo, h_hi = pl.ds(0, mid_h), pl.ds(mid_h, mid_h)

    def y_far(tag, buf):
        links.send(("half", tag, 0), buf.at[h_lo], half_in.at[tag, 0], north)
        links.send(("half", tag, 1), buf.at[h_hi], half_in.at[tag, 1], south)

    def y_near(tag, side, buf, value):
        links.arrived(("half", tag, side))
        extra = half_in[tag, side].astype(F32)
        if side == 0:
            buf[h_lo] = (value[:mid_h] + extra).astype(BF16)
            buf[h_hi] = value[mid_h:].astype(BF16)
        else:
            buf[h_lo] = value[:mid_h].astype(BF16)
            buf[h_hi] = (value[mid_h:] + extra).astype(BF16)
        links.send(("full", tag, side), buf, full_in.at[tag, side], (north, south)[side])

    def y_sum(tag, value):
        for side in (0, 1):
            links.arrived(("full", tag, side))
            value = value + full_in[tag, side].astype(F32)
        return value

    for dy in (2, 1, 3, 0):
        to_sibling(IN, 1, dy)
    for dx in (1, 0):
        to_sibling(OUT, dx, 2)
    take_pair(0, 4)
    for way in (BELOW, ABOVE):
        hop_back(way, 4)
    for n, dy in enumerate((2, 1, 3, 0)):
        part_in[1, dy] = chip_sum(IN, 1, dy).astype(BF16)
        links.send(("xl", IN, dy), part_in.at[1, dy], xl_in.at[dy], twin)
        if n < 2:
            dx = 1 - n
            part_out[dx, 2] = chip_sum(OUT, dx, 2).astype(BF16)
            y_far(dx, part_out.at[dx, 2])
    for dx in (1, 0):
        for dy in (1, 3):
            to_sibling(OUT, dx, dy)
    for way in (BELOW, ABOVE):
        take_pair(way, 3)
        take_in(way, 3)
        hop_back(way, 3)
    for dx in (1, 0):
        for side, dy in enumerate((1, 3)):
            y_near(dx, side, part_out.at[dx, dy], chip_sum(OUT, dx, dy))
    for dy in (2, 1, 3, 0):
        to_sibling(IN, 0, dy)
    for dx in (1, 0):
        to_sibling(OUT, dx, 0)

    def both_x(dy):
        value = chip_sum(IN, 0, dy)
        links.arrived(("xl", IN, dy))
        return value + xl_in[dy].astype(F32)

    part_in[0, 2] = both_x(2).astype(BF16)
    y_far(2, part_in.at[0, 2])
    for way in (BELOW, ABOVE):
        take_pair(way, 2)
        take_in(way, 2)
        hop_back(way, 2)
    part_out[1, 0] = y_sum(1, chip_sum(OUT, 1, 0)).astype(BF16)
    links.send(("xl", OUT), part_out.at[1, 0], xl_out, twin)
    for side, dy in enumerate((1, 3)):
        y_near(2, side, part_in.at[0, dy], both_x(dy))
    for way in (BELOW, ABOVE):
        take_pair(way, 1)
        take_in(way, 1)
        hop_back(way, 1)

    scale = 1.0 / math.sqrt(16 * 16 * SHARD)
    last = y_sum(0, chip_sum(OUT, 0, 0))
    links.arrived(("xl", OUT))
    gout_ref[...] = ((last + xl_out[...].astype(F32)) * scale).astype(BF16)

    take_pair(0, 0)
    for way in (BELOW, ABOVE):
        take_in(way, 0)
    at = pl.ds(row_of(PAIR, 0, 0), SHARD)
    links.send(("gx end",), gx.at[at, left], from_pair_end, pair)

    last = y_sum(2, both_x(0))
    gin_ref[...] = (last * scale).T.astype(BF16)

    at = pl.ds(row_of(OWN, 0, 0), SHARD)
    gtok_ref[:, right] = gx[at, right]
    links.arrived(("gx end",))
    gtok_ref[:, left] = (gx[at, left].astype(F32) + from_pair_end[...].astype(F32)).astype(BF16)

    links.finish()


def local(tokens, cotangent, w_in, w_out):
    width, hidden = w_in.shape
    block = width // 16
    group = 16 * SHARD
    vmem = pltpu.VMEM
    hbm = pl.BlockSpec(memory_space=pl.ANY)
    return pl.pallas_call(
        kernel,
        out_shape=(
            jax.ShapeDtypeStruct((SHARD, width), BF16),
            jax.ShapeDtypeStruct((block, hidden), BF16),
            jax.ShapeDtypeStruct((hidden, block), BF16),
        ),
        in_specs=[hbm] * 4,
        out_specs=(pl.BlockSpec(memory_space=pltpu.VMEM),) * 3,
        scratch_shapes=[
            vmem((group, width), BF16),
            vmem((group, width), BF16),
            vmem((width, hidden), BF16),
            vmem((hidden, width), BF16),
            vmem((group, hidden), BF16),
            vmem((hidden, group), BF16),
            vmem((hidden, group), BF16),
            vmem((group, width), BF16),
            vmem((3, 2, 4, SHARD, width // 2), BF16),
            vmem((8, SHARD, width // 2), BF16),
            vmem((SHARD, width // 2), BF16),
            vmem((2, 2, Y, hidden, block), BF16),
            vmem((2, 2, Y, hidden, block), BF16),
            vmem((2, Y, hidden, block), BF16),
            vmem((2, Y, hidden, block), BF16),
            vmem((Y, hidden, block), BF16),
            vmem((hidden, block), BF16),
            vmem((3, 2, hidden // 2, block), BF16),
            vmem((3, 2, hidden, block), BF16),
            pltpu.SemaphoreType.DMA((4,)),
            pltpu.SemaphoreType.DMA((MESSAGES,)),
            pltpu.SemaphoreType.DMA((MESSAGES,)),
        ],
        compiler_params=pltpu.CompilerParams(
            collective_id=0, has_side_effects=True, vmem_limit_bytes=60 * 2**20
        ),
        cost_estimate=pl.CostEstimate(
            flops=10 * group * width * hidden,
            bytes_accessed=4 * width * hidden,
            transcendentals=group * hidden,
        ),
    )(tokens, cotangent, w_in, w_out)


def solution(mesh):
    placed = (
        P(("dp", "tensor"), None),
        P(("dp", "tensor"), None),
        P(None, "tensor"),
        P("tensor", None),
    )
    return jax.shard_map(
        local,
        mesh=mesh,
        in_specs=placed,
        out_specs=(P(("dp", "tensor"), None), P("dp", "tensor"), P("tensor", "dp")),
        check_vma=False,
    )
```

```python
import functools
import math

import jax
import jax.numpy as jnp
from jax import lax
from jax.experimental import pallas as pl
from jax.experimental.pallas import tpu as pltpu
from jax.sharding import PartitionSpec as P

MESH = pl.DeviceIdType.MESH
F32, BF16 = jnp.float32, jnp.bfloat16
CUBIC, ROOT = 0.044715, 0.7978845608028654

SHARD = 32
HALF = SHARD // 2
CHUNK = 4 * SHARD
Z, Y = 8, 4
OWN, PAIR = 0, 1
BELOW, ABOVE = 0, 1


def gelu_parts(pre):
    tangent = jnp.tanh(ROOT * (pre + CUBIC * pre * pre * pre))
    value = 0.5 * pre * (1.0 + tangent)
    slope = 0.5 * (1.0 + tangent) + 0.5 * pre * (1.0 - tangent * tangent) * ROOT * (
        1.0 + 3.0 * CUBIC * pre * pre
    )
    return value, slope


def row_of(side, way, hop):
    if hop == 0:
        return 3 * CHUNK + side * SHARD
    if hop == 4:
        return 3 * CHUNK + (2 + side) * SHARD
    return (hop - 1) * CHUNK + (2 * way + side) * SHARD


class Links:
    def __init__(self, send_sems, recv_sems):
        self.send_sems, self.recv_sems = send_sems, recv_sems
        self.copies = {}

    def send(self, key, src, dst, device):
        at = len(self.copies)
        copy = pltpu.make_async_remote_copy(
            src_ref=src,
            dst_ref=dst,
            send_sem=self.send_sems.at[at],
            recv_sem=self.recv_sems.at[at],
            device_id=device,
            device_id_type=MESH,
        )
        copy.start()
        self.copies[key] = copy

    def arrived(self, key):
        self.copies[key].wait_recv()

    def finish(self):
        for copy in self.copies.values():
            copy.wait_send()


MESSAGES = 120
VMEM_LIMIT = 60 * 2**20


def kernel(
    tokens_ref, cotangent_ref, w_in_ref, w_out_ref,
    gtok_ref, gin_ref, gout_ref,
    tok, cot, win, wout, win_t, wout_t, slopes, dpre, actt, dpret, gx,
    from_z_left, from_z_right, from_pair, from_pair_end,
    core_out_in, core_in_in, core_out_out, core_in_out,
    part_in, part_out, xl_in, xl_out, half_in, full_in, half_out, full_out,
    local_sems, send_sems, recv_sems,
):
    width, hidden = w_in_ref.shape
    block = width // 16
    dp, tensor = lax.axis_index("dp"), lax.axis_index("tensor")
    xlo, y, core = dp // (2 * Y), (dp // 2) % Y, dp % 2
    z, xhi = tensor // 2, tensor % 2

    def device(xlo, y, core, z, xhi):
        return (xlo * (2 * Y) + y * 2 + core, z * 2 + xhi)

    up = device(xlo, y, core, (z + 1) % Z, xhi)
    down = device(xlo, y, core, (z + Z - 1) % Z, xhi)
    pair = device(1 - xlo, y, core, z, 1 - xhi)
    twin = device(1 - xlo, y, core, z, xhi)
    north = device(xlo, (y + 1) % Y, core, z, xhi)
    south = device(xlo, (y + Y - 1) % Y, core, z, xhi)
    sibling = device(xlo, y, 1 - core, z, xhi)
    everyone = (up, down, pair, twin, north, south, sibling)

    loads = [
        pltpu.make_async_copy(src, dst, local_sems.at[i])
        for i, (src, dst) in enumerate(
            (
                (tokens_ref, tok.at[pl.ds(row_of(OWN, 0, 0), SHARD)]),
                (cotangent_ref, cot.at[pl.ds(row_of(OWN, 0, 0), SHARD)]),
                (w_in_ref, win),
                (w_out_ref, wout),
            )
        )
    ]
    for load in loads:
        load.start()

    barrier = pltpu.get_barrier_semaphore()
    for other in everyone:
        pl.semaphore_signal(barrier, inc=1, device_id=other, device_id_type=MESH)
    pl.semaphore_wait(barrier, len(everyone))

    links = Links(send_sems, recv_sems)
    onward = {BELOW: up, ABOVE: down}

    def slot(buf, side, way, hop, part=slice(0, SHARD)):
        return buf.at[pl.ds(row_of(side, way, hop) + part.start, part.stop - part.start)]

    near_cols, far_cols = pl.ds(0, width - 512), pl.ds(width - 512, 512)

    def first_hop(name, src, buf, side):
        for way in (BELOW, ABOVE):
            dst = slot(buf, side, way, 1)
            if name == "x" and side == PAIR:
                src, dst = src.at[:, near_cols] if way == BELOW else src, dst.at[:, near_cols]
            links.send((name, side, way, 1), src, dst, onward[way])

    def travels(way, hop):
        if hop < 4:
            return slice(0, SHARD)
        return slice(0, HALF) if way == BELOW else slice(HALF, SHARD)

    def relay(name, buf, side, way, hop):
        part = travels(way, hop + 1)
        src, dst = slot(buf, side, way, hop, part), slot(buf, side, way, hop + 1, part)
        if name == "x" and side == PAIR:
            src, dst = src.at[:, near_cols], dst.at[:, near_cols]
        links.send((name, side, way, hop + 1), src, dst, onward[way])

    def dy_across(way, hop):
        part = travels(way, hop)
        links.send(
            ("dy", PAIR, way, hop),
            slot(cot, OWN, way, hop, part),
            slot(cot, PAIR, way, hop, part),
            pair,
        )

    def x_across(way, hop):
        part = travels(way, hop)
        links.send(
            ("x far", PAIR, way, hop),
            slot(tok, OWN, way, hop, part).at[:, far_cols],
            slot(tok, PAIR, way, hop, part).at[:, far_cols],
            pair,
        )

    links.send(("x", PAIR, 0, 0), tokens_ref, slot(tok, PAIR, 0, 0), pair)
    first_hop("dy", cotangent_ref, cot, OWN)
    first_hop("x", tokens_ref, tok, OWN)
    links.send(("dy", PAIR, 0, 0), cotangent_ref, slot(cot, PAIR, 0, 0), pair)
    loads[3].wait()

    def turn_out(j, carry):
        at = pl.ds(pl.multiple_of(j * 256, 256), 256)
        wout_t[at, :] = wout[:, at].T
        return carry

    lax.fori_loop(0, width // 256, turn_out, 0)
    links.arrived(("x", PAIR, 0, 0))
    first_hop("x", slot(tok, PAIR, 0, 0), tok, PAIR)

    def turn_in(j, carry):
        at = pl.ds(pl.multiple_of(j * 256, 256), 256)
        win_t[:, at] = win[at, :].T
        return carry

    def forward_x(chunk):
        rows = pl.ds(chunk * CHUNK, CHUNK)
        for n in range(0, hidden, 256):
            cols = pl.ds(n, 256)
            pre = jnp.dot(tok[rows, :], win[:, cols], preferred_element_type=F32)
            value, slope = gelu_parts(pre)
            slopes[:, cols] = slope
            actt[cols, rows] = value.T.astype(BF16)

    def forward_dy(chunk):
        rows = pl.ds(chunk * CHUNK, CHUNK)
        for n in range(0, hidden, 256):
            cols = pl.ds(n, 256)
            dact = jnp.dot(cot[rows, :], wout_t[:, cols], preferred_element_type=F32)
            change = dact * slopes[:, cols]
            dpre[rows, cols] = change.astype(BF16)
            dpret[cols, rows] = change.T.astype(BF16)

        def columns(j, carry):
            at = pl.ds(pl.multiple_of(j * 512, 512), 512)
            gx[rows, at] = jnp.dot(
                dpre[rows, :], win_t[:, at], preferred_element_type=F32
            ).astype(BF16)
            return carry

        lax.fori_loop(0, width // 512, columns, 0)

    mid = 7 * width // 16
    left, right = pl.ds(0, mid), pl.ds(mid, width - mid)

    def slot_id(way, hop):
        return 0 if hop == 0 else 7 if hop == 4 else 2 * hop - 1 + way

    def cross(way, hop):
        at = slot_id(way, hop)
        links.send(
            ("gx", PAIR, way, hop),
            gx.at[pl.ds(row_of(PAIR, way, hop), SHARD), right],
            from_pair.at[at],
            pair,
        )

    for hop in (1, 2, 3):
        for way in (BELOW, ABOVE):
            links.arrived(("dy", OWN, way, hop))
            relay("dy", cot, OWN, way, hop)
            dy_across(way, hop)
        for way in (BELOW, ABOVE):
            links.arrived(("x", OWN, way, hop))
            relay("x", tok, OWN, way, hop)
            x_across(way, hop)
        for way in (BELOW, ABOVE):
            links.arrived(("x", PAIR, way, hop))
            relay("x", tok, PAIR, way, hop)
        if hop == 1:
            for load in loads[:3]:
                load.wait()
            links.arrived(("dy", PAIR, 0, 0))
            lax.fori_loop(0, width // 256, turn_in, 0)
        else:
            for way in (BELOW, ABOVE):
                links.arrived(("x far", PAIR, way, hop - 1))
            forward_x(hop - 2)
            for way in (BELOW, ABOVE):
                links.arrived(("dy", PAIR, way, hop - 1))
            forward_dy(hop - 2)
    for way in (BELOW, ABOVE):
        links.arrived(("dy", OWN, way, 4))
        dy_across(way, 4)
    for way in (BELOW, ABOVE):
        links.arrived(("x far", PAIR, way, 3))
    forward_x(2)
    for way in (BELOW, ABOVE):
        links.arrived(("x", OWN, way, 4))
        x_across(way, 4)
    for way in (BELOW, ABOVE):
        links.arrived(("dy", PAIR, way, 3))
    forward_dy(2)
    for way in (BELOW, ABOVE):
        links.arrived(("x", PAIR, way, 4))
        links.arrived(("x far", PAIR, way, 4))
    forward_x(3)
    for way in (BELOW, ABOVE):
        links.arrived(("dy", PAIR, way, 4))
    forward_dy(3)

    back = {BELOW: down, ABOVE: up}
    pieces = ((PAIR, left), (OWN, left), (OWN, right))

    def add(dst, *others):
        total = dst[...].astype(F32)
        for other in others:
            total = total + other[...].astype(F32)
        dst[...] = total.astype(BF16)

    def landing(i, way, hop, part):
        rows = pl.ds(part.start, part.stop - part.start)
        if i == 2:
            return from_z_right.at[way, hop, rows]
        return from_z_left.at[i, way, hop, rows]

    def hop_back(i, way, hop):
        side, cols = pieces[i]
        part = travels(way, hop)
        links.send(
            ("gz", i, way, hop),
            slot(gx, side, way, hop, part).at[:, cols],
            landing(i, way, hop - 1, part),
            back[way],
        )

    def take_in(i, way, hop):
        side, cols = pieces[i]
        part = travels(way, hop + 1)
        links.arrived(("gz", i, way, hop + 1))
        add(slot(gx, side, way, hop, part).at[:, cols], landing(i, way, hop, part))

    def step_back(hop, *which):
        for i in which:
            for way in (BELOW, ABOVE):
                if i == 2:
                    take_pair(way, hop)
                take_in(i, way, hop)
                hop_back(i, way, hop)

    def take_pair(way, hop):
        links.arrived(("gx", PAIR, way, hop))
        add(
            gx.at[pl.ds(row_of(OWN, way, hop), SHARD), right],
            from_pair.at[slot_id(way, hop)],
        )

    cross(0, 4)
    for i in (0, 1):
        for way in (BELOW, ABOVE):
            hop_back(i, way, 4)
    for hop in (3, 2, 1):
        for way in (BELOW, ABOVE):
            cross(way, hop)
    cross(0, 0)

    IN, OUT = 0, 1
    cut = core_out_in.shape[2]
    core_out, core_in = (core_out_in, core_out_out), (core_in_in, core_in_out)

    def product(array, dx, dy, dc):
        there = ((xlo + dx) % 2) * (2 * Y) + ((y + dy) % Y) * 2 + (core + dc) % 2
        cols = pl.ds(pl.multiple_of(there * block, block), block)
        x, dy_cols = tok[:, cols], cot[:, cols]
        if array == IN:
            return (jnp.dot(dpret[:cut, :], x, preferred_element_type=F32),)
        return (
            jnp.dot(actt[...], dy_cols, preferred_element_type=F32),
            jnp.dot(dpret[cut:, :], x, preferred_element_type=F32),
        )

    def split(array):
        return ((0, cut),) if array == IN else ((0, hidden), (hidden, 2 * hidden - cut))

    def read(ref, array):
        return tuple(ref[a:b].astype(F32) for a, b in split(array))

    def write(ref, array, parts):
        for (a, b), part in zip(split(array), parts):
            ref[a:b] = part.astype(BF16)

    def plus(parts, others):
        return tuple(p + o for p, o in zip(parts, others))

    def to_sibling(array, dx, dy):
        write(core_out[array].at[dx, dy], array, product(array, dx, dy, 1))
        links.send(
            ("core", array, dx, dy),
            core_out[array].at[dx, dy],
            core_in[array].at[dx, dy],
            sibling,
        )

    def chip_sum(array, dx, dy):
        mine = product(array, dx, dy, 0)
        links.arrived(("core", array, dx, dy))
        return plus(mine, read(core_in[array].at[dx, dy], array))

    def half_of(tag):
        return half_in if tag == 2 else half_out.at[tag]

    def full_of(tag):
        return full_in if tag == 2 else full_out.at[tag]

    def y_far(tag, buf):
        rows = buf.shape[0] // 2
        for side, to in enumerate((north, south)):
            links.send(
                ("half", tag, side),
                buf.at[pl.ds(side * rows, rows)],
                half_of(tag).at[side],
                to,
            )

    def y_near(tag, side, buf, array, parts):
        write(buf, array, parts)
        links.arrived(("half", tag, side))
        rows = buf.shape[0] // 2
        add(buf.at[pl.ds(side * rows, rows)], half_of(tag).at[side])
        links.send(("full", tag, side), buf, full_of(tag).at[side], (north, south)[side])

    def y_sum(tag, array, parts):
        for side in (0, 1):
            links.arrived(("full", tag, side))
            parts = plus(parts, read(full_of(tag).at[side], array))
        return parts

    def x_first(dy):
        write(part_in.at[1, dy], IN, chip_sum(IN, 1, dy))
        links.send(("xl", IN, dy), part_in.at[1, dy], xl_in.at[dy], twin)

    def far_out(dx):
        write(part_out.at[dx, 2], OUT, chip_sum(OUT, dx, 2))
        y_far(dx, part_out.at[dx, 2])

    def near_out(dx):
        for side, dy in enumerate((1, 3)):
            y_near(dx, side, part_out.at[dx, dy], OUT, chip_sum(OUT, dx, dy))

    def both_x(dy):
        parts = chip_sum(IN, 0, dy)
        links.arrived(("xl", IN, dy))
        return plus(parts, read(xl_in.at[dy], IN))

    to_sibling(IN, 1, 2)
    to_sibling(IN, 1, 1)
    to_sibling(OUT, 1, 2)
    x_first(2)
    to_sibling(OUT, 0, 2)
    take_pair(0, 4)
    for way in (BELOW, ABOVE):
        hop_back(2, way, 4)
    far_out(1)
    to_sibling(IN, 1, 3)
    x_first(1)
    far_out(0)
    to_sibling(IN, 1, 0)
    x_first(3)
    step_back(3, 0)
    x_first(0)
    step_back(3, 1)
    for dx in (1, 0):
        to_sibling(OUT, dx, 1)
        to_sibling(OUT, dx, 3)
        if dx == 1:
            step_back(3, 2)
    for dy in (2, 1, 3, 0):
        to_sibling(IN, 0, dy)
    near_out(1)
    step_back(2, 0)
    write(part_in.at[0, 2], IN, both_x(2))
    y_far(2, part_in.at[0, 2])
    step_back(2, 1)
    near_out(0)
    for dx in (1, 0):
        to_sibling(OUT, dx, 0)
    step_back(2, 2)
    step_back(1, 0)
    write(part_out.at[1, 0], OUT, y_sum(1, OUT, chip_sum(OUT, 1, 0)))
    links.send(("xl", OUT), part_out.at[1, 0], xl_out, twin)
    step_back(1, 1)
    for side, dy in enumerate((1, 3)):
        y_near(2, side, part_in.at[0, dy], IN, both_x(dy))
    step_back(1, 2)

    at = pl.ds(row_of(PAIR, 0, 0), SHARD)
    for way in (BELOW, ABOVE):
        take_in(0, way, 0)
    links.send(("gx end",), gx.at[at, left], from_pair_end, pair)
    for way in (BELOW, ABOVE):
        take_in(1, way, 0)

    scale = 1.0 / math.sqrt(16 * 16 * SHARD)
    out_parts = y_sum(0, OUT, chip_sum(OUT, 0, 0))
    in_parts = both_x(0)
    take_pair(0, 0)
    for way in (BELOW, ABOVE):
        take_in(2, way, 0)
    at = pl.ds(row_of(OWN, 0, 0), SHARD)
    gtok_ref[:, right] = gx[at, right]
    links.arrived(("gx end",))
    gtok_ref[:, left] = (gx[at, left].astype(F32) + from_pair_end[...].astype(F32)).astype(BF16)

    links.arrived(("xl", OUT))
    grad_out, in_end = plus(out_parts, read(xl_out, OUT))
    gout_ref[...] = (grad_out * scale).astype(BF16)
    gin_ref[:, cut:] = (in_end * scale).T.astype(BF16)
    (in_start,) = y_sum(2, IN, in_parts)
    gin_ref[:, :cut] = (in_start * scale).T.astype(BF16)

    links.finish()


def hand_over(*refs):
    for src, dst in zip(refs[:3], refs[3:]):
        dst[...] = src[...]


def local(tokens, cotangent, w_in, w_out):
    results = layer(tokens, cotangent, w_in, w_out)
    return pl.pallas_call(
        hand_over,
        out_shape=tuple(jax.ShapeDtypeStruct(r.shape, r.dtype) for r in results),
        in_specs=[pl.BlockSpec(memory_space=pltpu.VMEM)] * 3,
        out_specs=(pl.BlockSpec(memory_space=pltpu.VMEM),) * 3,
    )(*results)


def layer(tokens, cotangent, w_in, w_out):
    width, hidden = w_in.shape
    block = width // 16
    group = 16 * SHARD
    mid = 7 * width // 16
    short, long = hidden - 64, hidden + 64
    vmem = pltpu.VMEM
    hbm = pl.BlockSpec(memory_space=pl.ANY)
    return pl.pallas_call(
        kernel,
        out_shape=(
            jax.ShapeDtypeStruct((SHARD, width), BF16),
            jax.ShapeDtypeStruct((block, hidden), BF16),
            jax.ShapeDtypeStruct((hidden, block), BF16),
        ),
        in_specs=[hbm] * 4,
        out_specs=(pl.BlockSpec(memory_space=pltpu.VMEM),) * 3,
        scratch_shapes=[
            vmem((group, width), BF16),
            vmem((group, width), BF16),
            vmem((width, hidden), BF16),
            vmem((hidden, width), BF16),
            vmem((hidden, width), BF16),
            vmem((width, hidden), BF16),
            vmem((CHUNK, hidden), F32),
            vmem((group, hidden), BF16),
            vmem((hidden, group), BF16),
            vmem((hidden, group), BF16),
            vmem((group, width), BF16),
            vmem((2, 2, 4, SHARD, mid), BF16),
            vmem((2, 4, SHARD, width - mid), BF16),
            vmem((8, SHARD, width - mid), BF16),
            vmem((SHARD, mid), BF16),
            vmem((2, Y, short, block), BF16),
            vmem((2, Y, short, block), BF16),
            vmem((2, Y, long, block), BF16),
            vmem((2, Y, long, block), BF16),
            vmem((2, Y, short, block), BF16),
            vmem((2, Y, long, block), BF16),
            vmem((Y, short, block), BF16),
            vmem((long, block), BF16),
            vmem((2, short // 2, block), BF16),
            vmem((2, short, block), BF16),
            vmem((2, 2, long // 2, block), BF16),
            vmem((2, 2, long, block), BF16),
            pltpu.SemaphoreType.DMA((4,)),
            pltpu.SemaphoreType.DMA((MESSAGES,)),
            pltpu.SemaphoreType.DMA((MESSAGES,)),
        ],
        compiler_params=pltpu.CompilerParams(
            collective_id=0, has_side_effects=True, vmem_limit_bytes=VMEM_LIMIT
        ),
        cost_estimate=pl.CostEstimate(
            flops=10 * group * width * hidden,
            bytes_accessed=4 * width * hidden,
            transcendentals=group * hidden,
        ),
    )(tokens, cotangent, w_in, w_out)


def solution(mesh):
    placed = (
        P(("dp", "tensor"), None),
        P(("dp", "tensor"), None),
        P(None, "tensor"),
        P("tensor", None),
    )
    return jax.shard_map(
        local,
        mesh=mesh,
        in_specs=placed,
        out_specs=(P(("dp", "tensor"), None), P("dp", "tensor"), P("tensor", "dp")),
        check_vma=False,
    )
```

```python
import functools
import math

import jax
import jax.numpy as jnp
from jax import lax
from jax.experimental import pallas as pl
from jax.experimental.pallas import tpu as pltpu
from jax.sharding import PartitionSpec as P

MESH = pl.DeviceIdType.MESH
F32, BF16 = jnp.float32, jnp.bfloat16
CUBIC, ROOT = 0.044715, 0.7978845608028654

SHARD = 32
HALF = SHARD // 2
CHUNK = 4 * SHARD
Z, Y = 8, 4
OWN, PAIR = 0, 1
BELOW, ABOVE = 0, 1


def gelu_parts(pre):
    tangent = jnp.tanh(ROOT * (pre + CUBIC * pre * pre * pre))
    value = 0.5 * pre * (1.0 + tangent)
    slope = 0.5 * (1.0 + tangent) + 0.5 * pre * (1.0 - tangent * tangent) * ROOT * (
        1.0 + 3.0 * CUBIC * pre * pre
    )
    return value, slope


def row_of(side, way, hop):
    if hop == 0:
        return 3 * CHUNK + side * SHARD
    if hop == 4:
        return 3 * CHUNK + (2 + side) * SHARD
    return (hop - 1) * CHUNK + (2 * way + side) * SHARD


class Links:
    def __init__(self, send_sems, recv_sems):
        self.send_sems, self.recv_sems = send_sems, recv_sems
        self.copies = {}

    def send(self, key, src, dst, device):
        at = len(self.copies)
        copy = pltpu.make_async_remote_copy(
            src_ref=src,
            dst_ref=dst,
            send_sem=self.send_sems.at[at],
            recv_sem=self.recv_sems.at[at],
            device_id=device,
            device_id_type=MESH,
        )
        copy.start()
        self.copies[key] = copy

    def arrived(self, key):
        self.copies[key].wait_recv()

    def finish(self):
        for copy in self.copies.values():
            copy.wait_send()


MESSAGES = 120
VMEM_LIMIT = 60 * 2**20


def kernel(
    tokens_ref, cotangent_ref, w_in_ref, w_out_ref,
    gtok_ref, gin_ref, gout_ref,
    tok, cot, win, wout, win_t, wout_t, dacts, dpre, actt, dpret, gx,
    from_z_left, from_z_right, from_pair, from_pair_end,
    core_out_in, core_in_in, core_out_out, core_in_out,
    part_in, part_out, xl_in, xl_out, half_in, full_in, half_out, full_out,
    local_sems, send_sems, recv_sems,
):
    width, hidden = w_in_ref.shape
    block = width // 16
    dp, tensor = lax.axis_index("dp"), lax.axis_index("tensor")
    xlo, y, core = dp // (2 * Y), (dp // 2) % Y, dp % 2
    z, xhi = tensor // 2, tensor % 2

    def device(xlo, y, core, z, xhi):
        return (xlo * (2 * Y) + y * 2 + core, z * 2 + xhi)

    up = device(xlo, y, core, (z + 1) % Z, xhi)
    down = device(xlo, y, core, (z + Z - 1) % Z, xhi)
    pair = device(1 - xlo, y, core, z, 1 - xhi)
    twin = device(1 - xlo, y, core, z, xhi)
    north = device(xlo, (y + 1) % Y, core, z, xhi)
    south = device(xlo, (y + Y - 1) % Y, core, z, xhi)
    sibling = device(xlo, y, 1 - core, z, xhi)
    everyone = (up, down, pair, twin, north, south, sibling)

    loads = [
        pltpu.make_async_copy(src, dst, local_sems.at[i])
        for i, (src, dst) in enumerate(
            (
                (tokens_ref, tok.at[pl.ds(row_of(OWN, 0, 0), SHARD)]),
                (cotangent_ref, cot.at[pl.ds(row_of(OWN, 0, 0), SHARD)]),
                (w_in_ref, win),
                (w_out_ref, wout),
            )
        )
    ]
    for load in loads:
        load.start()

    barrier = pltpu.get_barrier_semaphore()
    for other in everyone:
        pl.semaphore_signal(barrier, inc=1, device_id=other, device_id_type=MESH)
    pl.semaphore_wait(barrier, len(everyone))

    links = Links(send_sems, recv_sems)
    onward = {BELOW: up, ABOVE: down}

    def slot(buf, side, way, hop, part=slice(0, SHARD)):
        return buf.at[pl.ds(row_of(side, way, hop) + part.start, part.stop - part.start)]

    near_cols, far_cols = pl.ds(0, width - 512), pl.ds(width - 512, 512)

    def first_hop(name, src, buf):
        for way in (BELOW, ABOVE):
            links.send((name, OWN, way, 1), src, slot(buf, OWN, way, 1), onward[way])

    def travels(way, hop):
        if hop < 4:
            return slice(0, SHARD)
        return slice(0, HALF) if way == BELOW else slice(HALF, SHARD)

    def relay(name, buf, side, way, hop):
        part = travels(way, hop + 1)
        src, dst = slot(buf, side, way, hop, part), slot(buf, side, way, hop + 1, part)
        if name == "x" and side == PAIR:
            src, dst = src.at[:, near_cols], dst.at[:, near_cols]
        links.send((name, side, way, hop + 1), src, dst, onward[way])

    def dy_across(way, hop):
        part = travels(way, hop)
        links.send(
            ("dy", PAIR, way, hop),
            slot(cot, OWN, way, hop, part),
            slot(cot, PAIR, way, hop, part),
            pair,
        )

    def x_across(way, hop):
        part = travels(way, hop)
        links.send(
            ("x far", PAIR, way, hop),
            slot(tok, OWN, way, hop, part).at[:, far_cols],
            slot(tok, PAIR, way, hop, part).at[:, far_cols],
            pair,
        )

    links.send(("x", PAIR, 0, 0), tokens_ref, slot(tok, PAIR, 0, 0), pair)
    first_hop("dy", cotangent_ref, cot)
    first_hop("x", tokens_ref, tok)
    links.send(("dy", PAIR, 0, 0), cotangent_ref, slot(cot, PAIR, 0, 0), pair)
    loads[3].wait()

    def turn_out(j, carry):
        at = pl.ds(pl.multiple_of(j * 256, 256), 256)
        wout_t[at, :] = wout[:, at].T
        return carry

    lax.fori_loop(0, width // 256, turn_out, 0)
    links.arrived(("x", PAIR, 0, 0))
    for way in (BELOW, ABOVE):
        relay("x", tok, PAIR, way, 0)

    def turn_in(j, carry):
        at = pl.ds(pl.multiple_of(j * 256, 256), 256)
        win_t[:, at] = win[at, :].T
        return carry

    def forward_dy(chunk):
        rows = pl.ds(chunk * CHUNK, CHUNK)
        for n in range(0, hidden, 256):
            cols = pl.ds(n, 256)
            dacts[:, cols] = jnp.dot(cot[rows, :], wout_t[:, cols], preferred_element_type=F32)

    def forward_x(chunk):
        rows = pl.ds(chunk * CHUNK, CHUNK)
        for n in range(0, hidden, 256):
            cols = pl.ds(n, 256)
            pre = jnp.dot(tok[rows, :], win[:, cols], preferred_element_type=F32)
            value, slope = gelu_parts(pre)
            change = dacts[:, cols] * slope
            dpre[rows, cols] = change.astype(BF16)
            dpret[cols, rows] = change.T.astype(BF16)
            actt[cols, rows] = value.T.astype(BF16)

    def token_part(chunk):
        rows = pl.ds(chunk * CHUNK, CHUNK)

        def columns(j, carry):
            at = pl.ds(pl.multiple_of(j * 512, 512), 512)
            gx[rows, at] = jnp.dot(
                dpre[rows, :], win_t[:, at], preferred_element_type=F32
            ).astype(BF16)
            return carry

        lax.fori_loop(0, width // 512, columns, 0)

    mid = 7 * width // 16
    left, right = pl.ds(0, mid), pl.ds(mid, width - mid)

    def slot_id(way, hop):
        return 0 if hop == 0 else 7 if hop == 4 else 2 * hop - 1 + way

    def cross(way, hop):
        at = slot_id(way, hop)
        links.send(
            ("gx", PAIR, way, hop),
            gx.at[pl.ds(row_of(PAIR, way, hop), SHARD), right],
            from_pair.at[at],
            pair,
        )

    def dy_step(hop):
        for way in (BELOW, ABOVE):
            links.arrived(("dy", OWN, way, hop))
            if hop < 4:
                relay("dy", cot, OWN, way, hop)
            dy_across(way, hop)

    def x_step(hop):
        for way in (BELOW, ABOVE):
            links.arrived(("x", OWN, way, hop))
            if hop < 4:
                relay("x", tok, OWN, way, hop)
            x_across(way, hop)

    def all_arrived(name, hop):
        for way in (BELOW, ABOVE):
            links.arrived((name, PAIR, way, hop))

    def pair_relay(hop):
        for way in (BELOW, ABOVE):
            relay("x", tok, PAIR, way, hop)

    dy_step(1)
    x_step(1)
    all_arrived("x", 1)
    pair_relay(1)
    for load in loads[:3]:
        load.wait()
    links.arrived(("dy", PAIR, 0, 0))
    lax.fori_loop(0, width // 256, turn_in, 0)
    dy_step(2)
    x_step(2)
    all_arrived("dy", 1)
    forward_dy(0)
    all_arrived("x", 2)
    all_arrived("x far", 1)
    forward_x(0)
    token_part(0)
    dy_step(3)
    pair_relay(2)
    all_arrived("dy", 2)
    forward_dy(1)
    all_arrived("x far", 2)
    forward_x(1)
    x_step(3)
    dy_step(4)
    token_part(1)
    all_arrived("x", 3)
    pair_relay(3)
    all_arrived("dy", 3)
    forward_dy(2)
    all_arrived("x far", 3)
    forward_x(2)
    x_step(4)
    token_part(2)
    all_arrived("dy", 4)
    forward_dy(3)
    all_arrived("x", 4)
    all_arrived("x far", 4)
    forward_x(3)
    token_part(3)

    back = {BELOW: down, ABOVE: up}
    pieces = ((PAIR, left), (OWN, left), (OWN, right))

    def add(dst, *others):
        total = dst[...].astype(F32)
        for other in others:
            total = total + other[...].astype(F32)
        dst[...] = total.astype(BF16)

    def landing(i, way, hop, part):
        rows = pl.ds(part.start, part.stop - part.start)
        if i == 2:
            return from_z_right.at[way, hop, rows]
        return from_z_left.at[i, way, hop, rows]

    def hop_back(i, way, hop):
        side, cols = pieces[i]
        part = travels(way, hop)
        links.send(
            ("gz", i, way, hop),
            slot(gx, side, way, hop, part).at[:, cols],
            landing(i, way, hop - 1, part),
            back[way],
        )

    def take_in(i, way, hop):
        side, cols = pieces[i]
        part = travels(way, hop + 1)
        links.arrived(("gz", i, way, hop + 1))
        add(slot(gx, side, way, hop, part).at[:, cols], landing(i, way, hop, part))

    def step_back(hop, *which):
        for i in which:
            for way in (BELOW, ABOVE):
                if i == 2:
                    take_pair(way, hop)
                take_in(i, way, hop)
                hop_back(i, way, hop)

    def take_pair(way, hop):
        links.arrived(("gx", PAIR, way, hop))
        add(
            gx.at[pl.ds(row_of(OWN, way, hop), SHARD), right],
            from_pair.at[slot_id(way, hop)],
        )

    cross(0, 4)
    for i in (0, 1):
        for way in (BELOW, ABOVE):
            hop_back(i, way, 4)
    for hop in (3, 2, 1):
        for way in (BELOW, ABOVE):
            cross(way, hop)
    cross(0, 0)

    IN, OUT = 0, 1
    cut = core_out_in.shape[2]
    core_out, core_in = (core_out_in, core_out_out), (core_in_in, core_in_out)

    def product(array, dx, dy, dc):
        there = ((xlo + dx) % 2) * (2 * Y) + ((y + dy) % Y) * 2 + (core + dc) % 2
        cols = pl.ds(pl.multiple_of(there * block, block), block)
        x, dy_cols = tok[:, cols], cot[:, cols]
        if array == IN:
            return (jnp.dot(dpret[:cut, :], x, preferred_element_type=F32),)
        return (
            jnp.dot(actt[...], dy_cols, preferred_element_type=F32),
            jnp.dot(dpret[cut:, :], x, preferred_element_type=F32),
        )

    def split(array):
        return ((0, cut),) if array == IN else ((0, hidden), (hidden, 2 * hidden - cut))

    def read(ref, array):
        return tuple(ref[a:b].astype(F32) for a, b in split(array))

    def write(ref, array, parts):
        for (a, b), part in zip(split(array), parts):
            ref[a:b] = part.astype(BF16)

    def plus(parts, others):
        return tuple(p + o for p, o in zip(parts, others))

    def to_sibling(array, dx, dy):
        write(core_out[array].at[dx, dy], array, product(array, dx, dy, 1))
        links.send(
            ("core", array, dx, dy),
            core_out[array].at[dx, dy],
            core_in[array].at[dx, dy],
            sibling,
        )

    def chip_sum(array, dx, dy):
        mine = product(array, dx, dy, 0)
        links.arrived(("core", array, dx, dy))
        return plus(mine, read(core_in[array].at[dx, dy], array))

    def half_of(tag):
        return half_in if tag == 2 else half_out.at[tag]

    def full_of(tag):
        return full_in if tag == 2 else full_out.at[tag]

    def y_far(tag, buf):
        rows = buf.shape[0] // 2
        for side, to in enumerate((north, south)):
            links.send(
                ("half", tag, side),
                buf.at[pl.ds(side * rows, rows)],
                half_of(tag).at[side],
                to,
            )

    def y_near(tag, side, buf, array, parts):
        write(buf, array, parts)
        links.arrived(("half", tag, side))
        rows = buf.shape[0] // 2
        add(buf.at[pl.ds(side * rows, rows)], half_of(tag).at[side])
        links.send(("full", tag, side), buf, full_of(tag).at[side], (north, south)[side])

    def y_sum(tag, array, parts):
        for side in (0, 1):
            links.arrived(("full", tag, side))
            parts = plus(parts, read(full_of(tag).at[side], array))
        return parts

    def x_first(dy):
        write(part_in.at[1, dy], IN, chip_sum(IN, 1, dy))
        links.send(("xl", IN, dy), part_in.at[1, dy], xl_in.at[dy], twin)

    def far_out(dx):
        write(part_out.at[dx, 2], OUT, chip_sum(OUT, dx, 2))
        y_far(dx, part_out.at[dx, 2])

    def near_out(dx):
        for side, dy in enumerate((1, 3)):
            y_near(dx, side, part_out.at[dx, dy], OUT, chip_sum(OUT, dx, dy))

    def both_x(dy):
        parts = chip_sum(IN, 0, dy)
        links.arrived(("xl", IN, dy))
        return plus(parts, read(xl_in.at[dy], IN))

    to_sibling(OUT, 1, 2)
    to_sibling(IN, 1, 2)
    to_sibling(OUT, 0, 2)
    to_sibling(IN, 1, 1)
    far_out(1)
    x_first(2)
    far_out(0)
    x_first(1)
    to_sibling(IN, 1, 3)
    to_sibling(IN, 1, 0)
    step_back(3, 0)
    x_first(3)
    step_back(3, 1)
    x_first(0)
    take_pair(0, 4)
    for way in (BELOW, ABOVE):
        hop_back(2, way, 4)
    for dx in (1, 0):
        for dy in (1, 3):
            to_sibling(OUT, dx, dy)
    for dy in (2, 1, 3, 0):
        to_sibling(IN, 0, dy)
    near_out(1)
    step_back(2, 0)
    step_back(3, 2)
    write(part_in.at[0, 2], IN, both_x(2))
    y_far(2, part_in.at[0, 2])
    step_back(2, 1)
    near_out(0)
    for dx in (1, 0):
        to_sibling(OUT, dx, 0)
    step_back(2, 2)
    step_back(1, 0)
    write(part_out.at[1, 0], OUT, y_sum(1, OUT, chip_sum(OUT, 1, 0)))
    links.send(("xl", OUT), part_out.at[1, 0], xl_out, twin)
    step_back(1, 1)
    for side, dy in enumerate((1, 3)):
        y_near(2, side, part_in.at[0, dy], IN, both_x(dy))
    step_back(1, 2)

    at = pl.ds(row_of(PAIR, 0, 0), SHARD)
    for way in (BELOW, ABOVE):
        take_in(0, way, 0)
    links.send(("gx end",), gx.at[at, left], from_pair_end, pair)
    for way in (BELOW, ABOVE):
        take_in(1, way, 0)

    scale = 1.0 / math.sqrt(16 * 16 * SHARD)
    out_parts = y_sum(0, OUT, chip_sum(OUT, 0, 0))
    in_parts = both_x(0)
    take_pair(0, 0)
    for way in (BELOW, ABOVE):
        take_in(2, way, 0)
    at = pl.ds(row_of(OWN, 0, 0), SHARD)
    gtok_ref[:, right] = gx[at, right]
    links.arrived(("gx end",))
    gtok_ref[:, left] = (gx[at, left].astype(F32) + from_pair_end[...].astype(F32)).astype(BF16)

    links.arrived(("xl", OUT))
    grad_out, in_end = plus(out_parts, read(xl_out, OUT))
    gout_ref[...] = (grad_out * scale).astype(BF16)
    gin_ref[:, cut:] = (in_end * scale).T.astype(BF16)
    (in_start,) = y_sum(2, IN, in_parts)
    gin_ref[:, :cut] = (in_start * scale).T.astype(BF16)

    links.finish()


def hand_over(*refs):
    for src, dst in zip(refs[:3], refs[3:]):
        dst[...] = src[...]


def local(tokens, cotangent, w_in, w_out):
    return layer(tokens, cotangent, w_in, w_out)


def layer(tokens, cotangent, w_in, w_out):
    width, hidden = w_in.shape
    block = width // 16
    group = 16 * SHARD
    mid = 7 * width // 16
    short, long = hidden - 64, hidden + 64
    vmem = pltpu.VMEM
    hbm = pl.BlockSpec(memory_space=pl.ANY)
    return pl.pallas_call(
        kernel,
        out_shape=(
            vmem((SHARD, width), BF16),
            vmem((block, hidden), BF16),
            vmem((hidden, block), BF16),
        ),
        in_specs=[hbm] * 4,
        out_specs=(pl.BlockSpec(memory_space=pltpu.VMEM),) * 3,
        scratch_shapes=[
            vmem((group, width), BF16),
            vmem((group, width), BF16),
            vmem((width, hidden), BF16),
            vmem((hidden, width), BF16),
            vmem((hidden, width), BF16),
            vmem((width, hidden), BF16),
            vmem((CHUNK, hidden), F32),
            vmem((group, hidden), BF16),
            vmem((hidden, group), BF16),
            vmem((hidden, group), BF16),
            vmem((group, width), BF16),
            vmem((2, 2, 4, SHARD, mid), BF16),
            vmem((2, 4, SHARD, width - mid), BF16),
            vmem((8, SHARD, width - mid), BF16),
            vmem((SHARD, mid), BF16),
            vmem((2, Y, short, block), BF16),
            vmem((2, Y, short, block), BF16),
            vmem((2, Y, long, block), BF16),
            vmem((2, Y, long, block), BF16),
            vmem((2, Y, short, block), BF16),
            vmem((2, Y, long, block), BF16),
            vmem((Y, short, block), BF16),
            vmem((long, block), BF16),
            vmem((2, short // 2, block), BF16),
            vmem((2, short, block), BF16),
            vmem((2, 2, long // 2, block), BF16),
            vmem((2, 2, long, block), BF16),
            pltpu.SemaphoreType.DMA((4,)),
            pltpu.SemaphoreType.DMA((MESSAGES,)),
            pltpu.SemaphoreType.DMA((MESSAGES,)),
        ],
        compiler_params=pltpu.CompilerParams(
            collective_id=0, has_side_effects=True, vmem_limit_bytes=VMEM_LIMIT
        ),
        cost_estimate=pl.CostEstimate(
            flops=10 * group * width * hidden,
            bytes_accessed=4 * width * hidden,
            transcendentals=group * hidden,
        ),
    )(tokens, cotangent, w_in, w_out)


def solution(mesh):
    placed = (
        P(("dp", "tensor"), None),
        P(("dp", "tensor"), None),
        P(None, "tensor"),
        P("tensor", None),
    )
    return jax.shard_map(
        local,
        mesh=mesh,
        in_specs=placed,
        out_specs=(P(("dp", "tensor"), None), P("dp", "tensor"), P("tensor", "dp")),
        check_vma=False,
    )
```

```python
import functools
import math

import jax
import jax.numpy as jnp
from jax import lax
from jax.experimental import pallas as pl
from jax.experimental.pallas import tpu as pltpu
from jax.sharding import PartitionSpec as P

MESH = pl.DeviceIdType.MESH
F32, BF16 = jnp.float32, jnp.bfloat16
CUBIC, ROOT = 0.044715, 0.7978845608028654

SHARD = 32
HALF = SHARD // 2
CHUNK = 4 * SHARD
Z, Y = 8, 4
FAR = 512
OWN, PAIR = 0, 1
BELOW, ABOVE = 0, 1


def gelu_parts(pre):
    tangent = jnp.tanh(ROOT * (pre + CUBIC * pre * pre * pre))
    value = 0.5 * pre * (1.0 + tangent)
    slope = 0.5 * (1.0 + tangent) + 0.5 * pre * (1.0 - tangent * tangent) * ROOT * (
        1.0 + 3.0 * CUBIC * pre * pre
    )
    return value, slope


def row_of(side, way, hop):
    if hop == 0:
        return 3 * CHUNK + side * SHARD
    if hop == 4:
        return 3 * CHUNK + (2 + side) * SHARD
    return (hop - 1) * CHUNK + (2 * way + side) * SHARD


class Links:
    def __init__(self, send_sems, recv_sems):
        self.send_sems, self.recv_sems = send_sems, recv_sems
        self.copies = {}

    def send(self, key, src, dst, device):
        at = len(self.copies)
        copy = pltpu.make_async_remote_copy(
            src_ref=src,
            dst_ref=dst,
            send_sem=self.send_sems.at[at],
            recv_sem=self.recv_sems.at[at],
            device_id=device,
            device_id_type=MESH,
        )
        copy.start()
        self.copies[key] = copy

    def arrived(self, key):
        self.copies[key].wait_recv()

    def finish(self):
        for copy in self.copies.values():
            copy.wait_send()


MESSAGES = 120
VMEM_LIMIT = 60 * 2**20


def kernel(
    tokens_ref, cotangent_ref, w_in_ref, w_out_ref,
    gtok_ref, gin_ref, gout_ref,
    tok, cot, win, wout, win_t, wout_t, dacts, dpre, actt, dpret, gx,
    from_z_left, from_z_right, from_pair, from_pair_end,
    core_out_in, core_in_in, core_out_out, core_in_out,
    part_in, part_out, xl_in, xl_out, half_in, full_in, half_out, full_out,
    local_sems, send_sems, recv_sems,
):
    width, hidden = w_in_ref.shape
    block = width // 16
    dp, tensor = lax.axis_index("dp"), lax.axis_index("tensor")
    xlo, y, core = dp // (2 * Y), (dp // 2) % Y, dp % 2
    z, xhi = tensor // 2, tensor % 2

    def device(xlo, y, core, z, xhi):
        return (xlo * (2 * Y) + y * 2 + core, z * 2 + xhi)

    up = device(xlo, y, core, (z + 1) % Z, xhi)
    down = device(xlo, y, core, (z + Z - 1) % Z, xhi)
    pair = device(1 - xlo, y, core, z, 1 - xhi)
    twin = device(1 - xlo, y, core, z, xhi)
    north = device(xlo, (y + 1) % Y, core, z, xhi)
    south = device(xlo, (y + Y - 1) % Y, core, z, xhi)
    sibling = device(xlo, y, 1 - core, z, xhi)
    everyone = (up, down, pair, twin, north, south, sibling)

    loads = [
        pltpu.make_async_copy(src, dst, local_sems.at[i])
        for i, (src, dst) in enumerate(
            (
                (tokens_ref, tok.at[pl.ds(row_of(OWN, 0, 0), SHARD)]),
                (cotangent_ref, cot.at[pl.ds(row_of(OWN, 0, 0), SHARD)]),
                (w_in_ref, win),
                (w_out_ref, wout),
            )
        )
    ]
    for load in loads:
        load.start()

    barrier = pltpu.get_barrier_semaphore()
    for other in everyone:
        pl.semaphore_signal(barrier, inc=1, device_id=other, device_id_type=MESH)
    pl.semaphore_wait(barrier, len(everyone))

    links = Links(send_sems, recv_sems)
    onward = {BELOW: up, ABOVE: down}

    def slot(buf, side, way, hop, part=slice(0, SHARD)):
        return buf.at[pl.ds(row_of(side, way, hop) + part.start, part.stop - part.start)]

    near_cols, far_cols = pl.ds(0, width - FAR), pl.ds(width - FAR, FAR)

    def first_hop(name, src, buf):
        for way in (BELOW, ABOVE):
            links.send((name, OWN, way, 1), src, slot(buf, OWN, way, 1), onward[way])

    def travels(way, hop):
        if hop < 4:
            return slice(0, SHARD)
        return slice(0, HALF) if way == BELOW else slice(HALF, SHARD)

    def relay(name, buf, side, way, hop):
        part = travels(way, hop + 1)
        src, dst = slot(buf, side, way, hop, part), slot(buf, side, way, hop + 1, part)
        if name == "x" and side == PAIR:
            src, dst = src.at[:, near_cols], dst.at[:, near_cols]
        links.send((name, side, way, hop + 1), src, dst, onward[way])

    def dy_across(way, hop):
        part = travels(way, hop)
        links.send(
            ("dy", PAIR, way, hop),
            slot(cot, OWN, way, hop, part),
            slot(cot, PAIR, way, hop, part),
            pair,
        )

    def x_across(way, hop):
        part = travels(way, hop)
        links.send(
            ("x far", PAIR, way, hop),
            slot(tok, OWN, way, hop, part).at[:, far_cols],
            slot(tok, PAIR, way, hop, part).at[:, far_cols],
            pair,
        )

    links.send(("x", PAIR, 0, 0), tokens_ref, slot(tok, PAIR, 0, 0), pair)
    first_hop("dy", cotangent_ref, cot)
    first_hop("x", tokens_ref, tok)
    links.send(("dy", PAIR, 0, 0), cotangent_ref, slot(cot, PAIR, 0, 0), pair)
    loads[3].wait()

    def turn_out(j, carry):
        at = pl.ds(pl.multiple_of(j * 256, 256), 256)
        wout_t[at, :] = wout[:, at].T
        return carry

    lax.fori_loop(0, width // 256, turn_out, 0)
    links.arrived(("x", PAIR, 0, 0))
    for way in (BELOW, ABOVE):
        relay("x", tok, PAIR, way, 0)

    def turn_in(j, carry):
        at = pl.ds(pl.multiple_of(j * 256, 256), 256)
        win_t[:, at] = win[at, :].T
        return carry

    def forward_dy(chunk):
        rows = pl.ds(chunk * CHUNK, CHUNK)
        for n in range(0, hidden, 256):
            cols = pl.ds(n, 256)
            dacts[:, cols] = jnp.dot(cot[rows, :], wout_t[:, cols], preferred_element_type=F32)

    def forward_x(chunk):
        rows = pl.ds(chunk * CHUNK, CHUNK)
        for n in range(0, hidden, 256):
            cols = pl.ds(n, 256)
            pre = jnp.dot(tok[rows, :], win[:, cols], preferred_element_type=F32)
            value, slope = gelu_parts(pre)
            change = dacts[:, cols] * slope
            dpre[rows, cols] = change.astype(BF16)
            dpret[cols, rows] = change.T.astype(BF16)
            actt[cols, rows] = value.T.astype(BF16)

    def token_part(chunk):
        rows = pl.ds(chunk * CHUNK, CHUNK)

        def columns(j, carry):
            at = pl.ds(pl.multiple_of(j * 512, 512), 512)
            gx[rows, at] = jnp.dot(
                dpre[rows, :], win_t[:, at], preferred_element_type=F32
            ).astype(BF16)
            return carry

        lax.fori_loop(0, width // 512, columns, 0)

    mid = 7 * width // 16
    left, right = pl.ds(0, mid), pl.ds(mid, width - mid)

    def slot_id(way, hop):
        return 0 if hop == 0 else 7 if hop == 4 else 2 * hop - 1 + way

    def cross(way, hop):
        at = slot_id(way, hop)
        links.send(
            ("gx", PAIR, way, hop),
            gx.at[pl.ds(row_of(PAIR, way, hop), SHARD), right],
            from_pair.at[at],
            pair,
        )

    def dy_step(hop):
        for way in (BELOW, ABOVE):
            links.arrived(("dy", OWN, way, hop))
            if hop < 4:
                relay("dy", cot, OWN, way, hop)
            dy_across(way, hop)

    def x_step(hop):
        for way in (BELOW, ABOVE):
            links.arrived(("x", OWN, way, hop))
            if hop < 4:
                relay("x", tok, OWN, way, hop)
            x_across(way, hop)

    def all_arrived(name, hop):
        for way in (BELOW, ABOVE):
            links.arrived((name, PAIR, way, hop))

    def pair_relay(hop):
        for way in (BELOW, ABOVE):
            relay("x", tok, PAIR, way, hop)

    dy_step(1)
    x_step(1)
    all_arrived("x", 1)
    pair_relay(1)
    for load in loads[:3]:
        load.wait()
    links.arrived(("dy", PAIR, 0, 0))
    lax.fori_loop(0, width // 256, turn_in, 0)
    dy_step(2)
    x_step(2)
    all_arrived("dy", 1)
    forward_dy(0)
    all_arrived("x", 2)
    all_arrived("x far", 1)
    forward_x(0)
    token_part(0)
    dy_step(3)
    pair_relay(2)
    all_arrived("dy", 2)
    forward_dy(1)
    all_arrived("x far", 2)
    forward_x(1)
    x_step(3)
    dy_step(4)
    token_part(1)
    all_arrived("x", 3)
    pair_relay(3)
    all_arrived("dy", 3)
    forward_dy(2)
    all_arrived("x far", 3)
    forward_x(2)
    x_step(4)
    token_part(2)
    all_arrived("dy", 4)
    forward_dy(3)
    all_arrived("x", 4)
    all_arrived("x far", 4)
    forward_x(3)

    back = {BELOW: down, ABOVE: up}
    pieces = ((PAIR, left), (OWN, left), (OWN, right))

    def add(dst, *others):
        total = dst[...].astype(F32)
        for other in others:
            total = total + other[...].astype(F32)
        dst[...] = total.astype(BF16)

    def landing(i, way, hop, part):
        rows = pl.ds(part.start, part.stop - part.start)
        if i == 2:
            return from_z_right.at[way, hop, rows]
        return from_z_left.at[i, way, hop, rows]

    def hop_back(i, way, hop):
        side, cols = pieces[i]
        part = travels(way, hop)
        links.send(
            ("gz", i, way, hop),
            slot(gx, side, way, hop, part).at[:, cols],
            landing(i, way, hop - 1, part),
            back[way],
        )

    def take_in(i, way, hop):
        side, cols = pieces[i]
        part = travels(way, hop + 1)
        links.arrived(("gz", i, way, hop + 1))
        add(slot(gx, side, way, hop, part).at[:, cols], landing(i, way, hop, part))

    def step_back(hop, *which):
        for i in which:
            for way in (BELOW, ABOVE):
                if i == 2:
                    take_pair(way, hop)
                take_in(i, way, hop)
                hop_back(i, way, hop)

    def take_pair(way, hop):
        links.arrived(("gx", PAIR, way, hop))
        add(
            gx.at[pl.ds(row_of(OWN, way, hop), SHARD), right],
            from_pair.at[slot_id(way, hop)],
        )

    IN, OUT = 0, 1
    cut = core_out_in.shape[2]
    core_out, core_in = (core_out_in, core_out_out), (core_in_in, core_in_out)

    def product(array, dx, dy, dc):
        there = ((xlo + dx) % 2) * (2 * Y) + ((y + dy) % Y) * 2 + (core + dc) % 2
        cols = pl.ds(pl.multiple_of(there * block, block), block)
        x, dy_cols = tok[:, cols], cot[:, cols]
        if array == IN:
            return (jnp.dot(dpret[:cut, :], x, preferred_element_type=F32),)
        return (
            jnp.dot(actt[...], dy_cols, preferred_element_type=F32),
            jnp.dot(dpret[cut:, :], x, preferred_element_type=F32),
        )

    def split(array):
        return ((0, cut),) if array == IN else ((0, hidden), (hidden, 2 * hidden - cut))

    def read(ref, array):
        return tuple(ref[a:b].astype(F32) for a, b in split(array))

    def write(ref, array, parts):
        for (a, b), part in zip(split(array), parts):
            ref[a:b] = part.astype(BF16)

    def plus(parts, others):
        return tuple(p + o for p, o in zip(parts, others))

    def to_sibling(array, dx, dy):
        write(core_out[array].at[dx, dy], array, product(array, dx, dy, 1))
        links.send(
            ("core", array, dx, dy),
            core_out[array].at[dx, dy],
            core_in[array].at[dx, dy],
            sibling,
        )

    def chip_sum(array, dx, dy):
        mine = product(array, dx, dy, 0)
        links.arrived(("core", array, dx, dy))
        return plus(mine, read(core_in[array].at[dx, dy], array))

    def half_of(tag):
        return half_in if tag == 2 else half_out.at[tag]

    def full_of(tag):
        return full_in if tag == 2 else full_out.at[tag]

    def y_far(tag, buf):
        rows = buf.shape[0] // 2
        for side, to in enumerate((north, south)):
            links.send(
                ("half", tag, side),
                buf.at[pl.ds(side * rows, rows)],
                half_of(tag).at[side],
                to,
            )

    def y_near(tag, side, buf, array, parts):
        write(buf, array, parts)
        links.arrived(("half", tag, side))
        rows = buf.shape[0] // 2
        add(buf.at[pl.ds(side * rows, rows)], half_of(tag).at[side])
        links.send(("full", tag, side), buf, full_of(tag).at[side], (north, south)[side])

    def y_sum(tag, array, parts):
        for side in (0, 1):
            links.arrived(("full", tag, side))
            parts = plus(parts, read(full_of(tag).at[side], array))
        return parts

    def x_first(dy):
        write(part_in.at[1, dy], IN, chip_sum(IN, 1, dy))
        links.send(("xl", IN, dy), part_in.at[1, dy], xl_in.at[dy], twin)

    def far_out(dx):
        write(part_out.at[dx, 2], OUT, chip_sum(OUT, dx, 2))
        y_far(dx, part_out.at[dx, 2])

    def near_out(dx):
        for side, dy in enumerate((1, 3)):
            y_near(dx, side, part_out.at[dx, dy], OUT, chip_sum(OUT, dx, dy))

    def both_x(dy):
        parts = chip_sum(IN, 0, dy)
        links.arrived(("xl", IN, dy))
        return plus(parts, read(xl_in.at[dy], IN))

    to_sibling(OUT, 1, 2)
    to_sibling(IN, 1, 2)
    token_part(3)
    cross(0, 4)
    for i in (0, 1):
        for way in (BELOW, ABOVE):
            hop_back(i, way, 4)
    far_out(1)
    to_sibling(OUT, 0, 2)
    x_first(2)
    for hop in (3, 2, 1):
        for way in (BELOW, ABOVE):
            cross(way, hop)
    cross(0, 0)
    to_sibling(IN, 1, 1)
    far_out(0)
    to_sibling(IN, 1, 3)
    x_first(1)
    to_sibling(IN, 1, 0)
    step_back(3, 0)
    x_first(3)
    take_pair(0, 4)
    for way in (BELOW, ABOVE):
        hop_back(2, way, 4)
    step_back(3, 1)
    x_first(0)
    for dx in (1, 0):
        for dy in (1, 3):
            to_sibling(OUT, dx, dy)
    to_sibling(IN, 0, 2)
    near_out(1)
    for dy in (1, 3, 0):
        to_sibling(IN, 0, dy)
    step_back(2, 0)
    step_back(3, 2)
    write(part_in.at[0, 2], IN, both_x(2))
    y_far(2, part_in.at[0, 2])
    step_back(2, 1)
    near_out(0)
    for dx in (1, 0):
        to_sibling(OUT, dx, 0)
    step_back(1, 0)
    write(part_out.at[1, 0], OUT, y_sum(1, OUT, chip_sum(OUT, 1, 0)))
    links.send(("xl", OUT), part_out.at[1, 0], xl_out, twin)
    step_back(2, 2)
    for side, dy in enumerate((1, 3)):
        y_near(2, side, part_in.at[0, dy], IN, both_x(dy))
    step_back(1, 1)

    at = pl.ds(row_of(PAIR, 0, 0), SHARD)
    for way in (BELOW, ABOVE):
        take_in(0, way, 0)
    links.send(("gx end",), gx.at[at, left], from_pair_end, pair)
    step_back(1, 2)
    for way in (BELOW, ABOVE):
        take_in(1, way, 0)

    scale = 1.0 / math.sqrt(16 * 16 * SHARD)
    out_parts = y_sum(0, OUT, chip_sum(OUT, 0, 0))
    in_parts = both_x(0)
    take_pair(0, 0)
    for way in (BELOW, ABOVE):
        take_in(2, way, 0)
    at = pl.ds(row_of(OWN, 0, 0), SHARD)
    gtok_ref[:, right] = gx[at, right]
    links.arrived(("gx end",))
    gtok_ref[:, left] = (gx[at, left].astype(F32) + from_pair_end[...].astype(F32)).astype(BF16)

    links.arrived(("xl", OUT))
    grad_out, in_end = plus(out_parts, read(xl_out, OUT))
    gout_ref[...] = (grad_out * scale).astype(BF16)
    gin_ref[:, cut:] = (in_end * scale).T.astype(BF16)
    (in_start,) = y_sum(2, IN, in_parts)
    gin_ref[:, :cut] = (in_start * scale).T.astype(BF16)

    links.finish()


def hand_over(*refs):
    for src, dst in zip(refs[:3], refs[3:]):
        dst[...] = src[...]


def local(tokens, cotangent, w_in, w_out):
    return layer(tokens, cotangent, w_in, w_out)


def layer(tokens, cotangent, w_in, w_out):
    width, hidden = w_in.shape
    block = width // 16
    group = 16 * SHARD
    mid = 7 * width // 16
    short, long = hidden - 64, hidden + 64
    vmem = pltpu.VMEM
    hbm = pl.BlockSpec(memory_space=pl.ANY)
    return pl.pallas_call(
        kernel,
        out_shape=(
            vmem((SHARD, width), BF16),
            vmem((block, hidden), BF16),
            vmem((hidden, block), BF16),
        ),
        in_specs=[hbm] * 4,
        out_specs=(pl.BlockSpec(memory_space=pltpu.VMEM),) * 3,
        scratch_shapes=[
            vmem((group, width), BF16),
            vmem((group, width), BF16),
            vmem((width, hidden), BF16),
            vmem((hidden, width), BF16),
            vmem((hidden, width), BF16),
            vmem((width, hidden), BF16),
            vmem((CHUNK, hidden), F32),
            vmem((group, hidden), BF16),
            vmem((hidden, group), BF16),
            vmem((hidden, group), BF16),
            vmem((group, width), BF16),
            vmem((2, 2, 4, SHARD, mid), BF16),
            vmem((2, 4, SHARD, width - mid), BF16),
            vmem((8, SHARD, width - mid), BF16),
            vmem((SHARD, mid), BF16),
            vmem((2, Y, short, block), BF16),
            vmem((2, Y, short, block), BF16),
            vmem((2, Y, long, block), BF16),
            vmem((2, Y, long, block), BF16),
            vmem((2, Y, short, block), BF16),
            vmem((2, Y, long, block), BF16),
            vmem((Y, short, block), BF16),
            vmem((long, block), BF16),
            vmem((2, short // 2, block), BF16),
            vmem((2, short, block), BF16),
            vmem((2, 2, long // 2, block), BF16),
            vmem((2, 2, long, block), BF16),
            pltpu.SemaphoreType.DMA((4,)),
            pltpu.SemaphoreType.DMA((MESSAGES,)),
            pltpu.SemaphoreType.DMA((MESSAGES,)),
        ],
        compiler_params=pltpu.CompilerParams(
            collective_id=0, has_side_effects=True, vmem_limit_bytes=VMEM_LIMIT
        ),
        cost_estimate=pl.CostEstimate(
            flops=10 * group * width * hidden,
            bytes_accessed=4 * width * hidden,
            transcendentals=group * hidden,
        ),
    )(tokens, cotangent, w_in, w_out)


def solution(mesh):
    placed = (
        P(("dp", "tensor"), None),
        P(("dp", "tensor"), None),
        P(None, "tensor"),
        P("tensor", None),
    )
    return jax.shard_map(
        local,
        mesh=mesh,
        in_specs=placed,
        out_specs=(P(("dp", "tensor"), None), P("dp", "tensor"), P("tensor", "dp")),
        check_vma=False,
    )
```

```python
import functools
import math

import jax
import jax.numpy as jnp
from jax import lax
from jax.experimental import pallas as pl
from jax.experimental.pallas import tpu as pltpu
from jax.sharding import PartitionSpec as P

MESH = pl.DeviceIdType.MESH
F32, BF16 = jnp.float32, jnp.bfloat16
CUBIC, ROOT = 0.044715, 0.7978845608028654

SHARD = 32
HALF = SHARD // 2
CHUNK = 4 * SHARD
Z, Y = 8, 4
FAR = 512
OWN, PAIR = 0, 1
BELOW, ABOVE = 0, 1


def gelu_parts(pre):
    tangent = jnp.tanh(ROOT * (pre + CUBIC * pre * pre * pre))
    value = 0.5 * pre * (1.0 + tangent)
    slope = 0.5 * (1.0 + tangent) + 0.5 * pre * (1.0 - tangent * tangent) * ROOT * (
        1.0 + 3.0 * CUBIC * pre * pre
    )
    return value, slope


def row_of(side, way, hop):
    if hop == 0:
        return 3 * CHUNK + side * SHARD
    if hop == 4:
        return 3 * CHUNK + (2 + side) * SHARD
    return (hop - 1) * CHUNK + (2 * way + side) * SHARD


class Links:
    def __init__(self, send_sems, recv_sems):
        self.send_sems, self.recv_sems = send_sems, recv_sems
        self.copies = {}

    def send(self, key, src, dst, device):
        at = len(self.copies)
        copy = pltpu.make_async_remote_copy(
            src_ref=src,
            dst_ref=dst,
            send_sem=self.send_sems.at[at],
            recv_sem=self.recv_sems.at[at],
            device_id=device,
            device_id_type=MESH,
        )
        copy.start()
        self.copies[key] = copy

    def arrived(self, key):
        self.copies[key].wait_recv()

    def finish(self):
        for copy in self.copies.values():
            copy.wait_send()


MESSAGES = 120
VMEM_LIMIT = 60 * 2**20


def kernel(
    tokens_ref, cotangent_ref, w_in_ref, w_out_ref,
    gtok_ref, gin_ref, gout_ref,
    tok, cot, win, wout, win_t, wout_t, dacts, dpre, actt, dpret, gx,
    from_z_left, from_z_right, from_pair, from_pair_end,
    core_out_in, core_in_in, core_out_out, core_in_out,
    part_in, part_out, xl_in, xl_out, half_in, full_in, half_out, full_out,
    local_sems, send_sems, recv_sems,
):
    width, hidden = w_in_ref.shape
    block = width // 16
    dp, tensor = lax.axis_index("dp"), lax.axis_index("tensor")
    xlo, y, core = dp // (2 * Y), (dp // 2) % Y, dp % 2
    z, xhi = tensor // 2, tensor % 2

    def device(xlo, y, core, z, xhi):
        return (xlo * (2 * Y) + y * 2 + core, z * 2 + xhi)

    up = device(xlo, y, core, (z + 1) % Z, xhi)
    down = device(xlo, y, core, (z + Z - 1) % Z, xhi)
    pair = device(1 - xlo, y, core, z, 1 - xhi)
    twin = device(1 - xlo, y, core, z, xhi)
    north = device(xlo, (y + 1) % Y, core, z, xhi)
    south = device(xlo, (y + Y - 1) % Y, core, z, xhi)
    sibling = device(xlo, y, 1 - core, z, xhi)
    everyone = (up, down, pair, twin, north, south, sibling)

    loads = [
        pltpu.make_async_copy(src, dst, local_sems.at[i])
        for i, (src, dst) in enumerate(
            (
                (tokens_ref, tok.at[pl.ds(row_of(OWN, 0, 0), SHARD)]),
                (cotangent_ref, cot.at[pl.ds(row_of(OWN, 0, 0), SHARD)]),
                (w_in_ref, win),
                (w_out_ref, wout),
            )
        )
    ]
    for load in loads:
        load.start()

    barrier = pltpu.get_barrier_semaphore()
    for other in everyone:
        pl.semaphore_signal(barrier, inc=1, device_id=other, device_id_type=MESH)
    pl.semaphore_wait(barrier, len(everyone))

    links = Links(send_sems, recv_sems)
    onward = {BELOW: up, ABOVE: down}

    def slot(buf, side, way, hop, part=slice(0, SHARD)):
        return buf.at[pl.ds(row_of(side, way, hop) + part.start, part.stop - part.start)]

    near_cols, far_cols = pl.ds(0, width - FAR), pl.ds(width - FAR, FAR)

    def first_hop(name, src, buf):
        for way in (BELOW, ABOVE):
            links.send((name, OWN, way, 1), src, slot(buf, OWN, way, 1), onward[way])

    def travels(way, hop):
        if hop < 4:
            return slice(0, SHARD)
        return slice(0, HALF) if way == BELOW else slice(HALF, SHARD)

    def relay(name, buf, side, way, hop):
        part = travels(way, hop + 1)
        src, dst = slot(buf, side, way, hop, part), slot(buf, side, way, hop + 1, part)
        if name == "x" and side == PAIR and hop < 3:
            src, dst = src.at[:, near_cols], dst.at[:, near_cols]
        links.send((name, side, way, hop + 1), src, dst, onward[way])

    def dy_across(way, hop):
        part = travels(way, hop)
        links.send(
            ("dy", PAIR, way, hop),
            slot(cot, OWN, way, hop, part),
            slot(cot, PAIR, way, hop, part),
            pair,
        )

    def x_across(way, hop):
        part = travels(way, hop)
        links.send(
            ("x far", PAIR, way, hop),
            slot(tok, OWN, way, hop, part).at[:, far_cols],
            slot(tok, PAIR, way, hop, part).at[:, far_cols],
            pair,
        )

    links.send(("x", PAIR, 0, 0), tokens_ref, slot(tok, PAIR, 0, 0), pair)
    first_hop("dy", cotangent_ref, cot)
    first_hop("x", tokens_ref, tok)
    links.send(("dy", PAIR, 0, 0), cotangent_ref, slot(cot, PAIR, 0, 0), pair)
    loads[3].wait()

    def turn_out(j, carry):
        at = pl.ds(pl.multiple_of(j * 256, 256), 256)
        wout_t[at, :] = wout[:, at].T
        return carry

    lax.fori_loop(0, width // 256, turn_out, 0)
    links.arrived(("x", PAIR, 0, 0))
    for way in (BELOW, ABOVE):
        relay("x", tok, PAIR, way, 0)

    def turn_in(j, carry):
        at = pl.ds(pl.multiple_of(j * 256, 256), 256)
        win_t[:, at] = win[at, :].T
        return carry

    def forward_dy(chunk):
        rows = pl.ds(chunk * CHUNK, CHUNK)
        for n in range(0, hidden, 256):
            cols = pl.ds(n, 256)
            dacts[:, cols] = jnp.dot(cot[rows, :], wout_t[:, cols], preferred_element_type=F32)

    def forward_x(chunk):
        rows = pl.ds(chunk * CHUNK, CHUNK)
        for n in range(0, hidden, 256):
            cols = pl.ds(n, 256)
            pre = jnp.dot(tok[rows, :], win[:, cols], preferred_element_type=F32)
            value, slope = gelu_parts(pre)
            change = dacts[:, cols] * slope
            dpre[rows, cols] = change.astype(BF16)
            dpret[cols, rows] = change.T.astype(BF16)
            actt[cols, rows] = value.T.astype(BF16)

    def token_part(chunk):
        rows = pl.ds(chunk * CHUNK, CHUNK)

        def columns(j, carry):
            at = pl.ds(pl.multiple_of(j * 512, 512), 512)
            gx[rows, at] = jnp.dot(
                dpre[rows, :], win_t[:, at], preferred_element_type=F32
            ).astype(BF16)
            return carry

        lax.fori_loop(0, width // 512, columns, 0)

    mid = 7 * width // 16
    left, right = pl.ds(0, mid), pl.ds(mid, width - mid)

    def slot_id(way, hop):
        return 0 if hop == 0 else 7 if hop == 4 else 2 * hop - 1 + way

    def cross(way, hop):
        at = slot_id(way, hop)
        links.send(
            ("gx", PAIR, way, hop),
            gx.at[pl.ds(row_of(PAIR, way, hop), SHARD), right],
            from_pair.at[at],
            pair,
        )

    def dy_step(hop):
        for way in (BELOW, ABOVE):
            links.arrived(("dy", OWN, way, hop))
            if hop < 4:
                relay("dy", cot, OWN, way, hop)
            dy_across(way, hop)

    def x_step(hop):
        for way in (BELOW, ABOVE):
            links.arrived(("x", OWN, way, hop))
            if hop < 4:
                relay("x", tok, OWN, way, hop)
                x_across(way, hop)

    def all_arrived(name, hop):
        for way in (BELOW, ABOVE):
            links.arrived((name, PAIR, way, hop))

    def pair_relay(hop):
        for way in (BELOW, ABOVE):
            relay("x", tok, PAIR, way, hop)

    dy_step(1)
    x_step(1)
    all_arrived("x", 1)
    for load in loads[:3]:
        load.wait()
    links.arrived(("dy", PAIR, 0, 0))
    lax.fori_loop(0, width // 256, turn_in, 0)
    dy_step(2)
    pair_relay(1)
    x_step(2)
    all_arrived("dy", 1)
    forward_dy(0)
    all_arrived("x far", 1)
    forward_x(0)
    token_part(0)
    dy_step(3)
    all_arrived("dy", 2)
    forward_dy(1)
    all_arrived("x", 2)
    pair_relay(2)
    all_arrived("x far", 2)
    forward_x(1)
    x_step(3)
    dy_step(4)
    token_part(1)
    all_arrived("x", 3)
    all_arrived("x far", 3)
    pair_relay(3)
    all_arrived("dy", 3)
    forward_dy(2)
    forward_x(2)
    token_part(2)
    all_arrived("dy", 4)
    forward_dy(3)
    x_step(4)
    all_arrived("x", 4)
    forward_x(3)

    back = {BELOW: down, ABOVE: up}
    pieces = ((PAIR, left), (OWN, left), (OWN, right))

    def add(dst, *others):
        total = dst[...].astype(F32)
        for other in others:
            total = total + other[...].astype(F32)
        dst[...] = total.astype(BF16)

    def landing(i, way, hop, part):
        rows = pl.ds(part.start, part.stop - part.start)
        if i == 2:
            return from_z_right.at[way, hop, rows]
        return from_z_left.at[i, way, hop, rows]

    def hop_back(i, way, hop):
        side, cols = pieces[i]
        part = travels(way, hop)
        links.send(
            ("gz", i, way, hop),
            slot(gx, side, way, hop, part).at[:, cols],
            landing(i, way, hop - 1, part),
            back[way],
        )

    def take_in(i, way, hop):
        side, cols = pieces[i]
        part = travels(way, hop + 1)
        links.arrived(("gz", i, way, hop + 1))
        add(slot(gx, side, way, hop, part).at[:, cols], landing(i, way, hop, part))

    def step_back(hop, *which):
        for i in which:
            for way in (BELOW, ABOVE):
                if i == 2:
                    take_pair(way, hop)
                take_in(i, way, hop)
                hop_back(i, way, hop)

    def take_pair(way, hop):
        links.arrived(("gx", PAIR, way, hop))
        add(
            gx.at[pl.ds(row_of(OWN, way, hop), SHARD), right],
            from_pair.at[slot_id(way, hop)],
        )

    IN, OUT = 0, 1
    cut = core_out_in.shape[2]
    core_out, core_in = (core_out_in, core_out_out), (core_in_in, core_in_out)

    def product(array, dx, dy, dc):
        there = ((xlo + dx) % 2) * (2 * Y) + ((y + dy) % Y) * 2 + (core + dc) % 2
        cols = pl.ds(pl.multiple_of(there * block, block), block)
        x, dy_cols = tok[:, cols], cot[:, cols]
        if array == IN:
            return (jnp.dot(dpret[:cut, :], x, preferred_element_type=F32),)
        return (
            jnp.dot(actt[...], dy_cols, preferred_element_type=F32),
            jnp.dot(dpret[cut:, :], x, preferred_element_type=F32),
        )

    def split(array):
        return ((0, cut),) if array == IN else ((0, hidden), (hidden, 2 * hidden - cut))

    def read(ref, array):
        return tuple(ref[a:b].astype(F32) for a, b in split(array))

    def write(ref, array, parts):
        for (a, b), part in zip(split(array), parts):
            ref[a:b] = part.astype(BF16)

    def plus(parts, others):
        return tuple(p + o for p, o in zip(parts, others))

    def to_sibling(array, dx, dy):
        write(core_out[array].at[dx, dy], array, product(array, dx, dy, 1))
        links.send(
            ("core", array, dx, dy),
            core_out[array].at[dx, dy],
            core_in[array].at[dx, dy],
            sibling,
        )

    def chip_sum(array, dx, dy):
        mine = product(array, dx, dy, 0)
        links.arrived(("core", array, dx, dy))
        return plus(mine, read(core_in[array].at[dx, dy], array))

    def half_of(tag):
        return half_in if tag == 2 else half_out.at[tag]

    def full_of(tag):
        return full_in if tag == 2 else full_out.at[tag]

    def y_far(tag, buf):
        rows = buf.shape[0] // 2
        for side, to in enumerate((north, south)):
            links.send(
                ("half", tag, side),
                buf.at[pl.ds(side * rows, rows)],
                half_of(tag).at[side],
                to,
            )

    def y_near(tag, side, buf, array, parts):
        write(buf, array, parts)
        links.arrived(("half", tag, side))
        rows = buf.shape[0] // 2
        add(buf.at[pl.ds(side * rows, rows)], half_of(tag).at[side])
        links.send(("full", tag, side), buf, full_of(tag).at[side], (north, south)[side])

    def y_sum(tag, array, parts):
        for side in (0, 1):
            links.arrived(("full", tag, side))
            parts = plus(parts, read(full_of(tag).at[side], array))
        return parts

    def x_first(dy):
        write(part_in.at[1, dy], IN, chip_sum(IN, 1, dy))
        links.send(("xl", IN, dy), part_in.at[1, dy], xl_in.at[dy], twin)

    def far_out(dx):
        write(part_out.at[dx, 2], OUT, chip_sum(OUT, dx, 2))
        y_far(dx, part_out.at[dx, 2])

    def near_out(dx):
        for side, dy in enumerate((1, 3)):
            y_near(dx, side, part_out.at[dx, dy], OUT, chip_sum(OUT, dx, dy))

    def both_x(dy):
        parts = chip_sum(IN, 0, dy)
        links.arrived(("xl", IN, dy))
        return plus(parts, read(xl_in.at[dy], IN))

    to_sibling(OUT, 1, 2)
    to_sibling(IN, 1, 2)
    token_part(3)
    cross(0, 4)
    for i in (0, 1):
        for way in (BELOW, ABOVE):
            hop_back(i, way, 4)
    far_out(1)
    to_sibling(OUT, 0, 2)
    x_first(2)
    for hop in (3, 2, 1):
        for way in (BELOW, ABOVE):
            cross(way, hop)
    cross(0, 0)
    to_sibling(IN, 1, 1)
    far_out(0)
    to_sibling(IN, 1, 3)
    x_first(1)
    to_sibling(IN, 1, 0)
    step_back(3, 0)
    x_first(3)
    take_pair(0, 4)
    for way in (BELOW, ABOVE):
        hop_back(2, way, 4)
    step_back(3, 1)
    x_first(0)
    for dx in (1, 0):
        for dy in (1, 3):
            to_sibling(OUT, dx, dy)
    to_sibling(IN, 0, 2)
    near_out(1)
    for dy in (1, 3, 0):
        to_sibling(IN, 0, dy)
    step_back(2, 0)
    step_back(3, 2)
    write(part_in.at[0, 2], IN, both_x(2))
    y_far(2, part_in.at[0, 2])
    step_back(2, 1)
    near_out(0)
    for dx in (1, 0):
        to_sibling(OUT, dx, 0)
    step_back(1, 0)
    write(part_out.at[1, 0], OUT, y_sum(1, OUT, chip_sum(OUT, 1, 0)))
    links.send(("xl", OUT), part_out.at[1, 0], xl_out, twin)
    step_back(2, 2)
    for side, dy in enumerate((1, 3)):
        y_near(2, side, part_in.at[0, dy], IN, both_x(dy))
    step_back(1, 1)

    at = pl.ds(row_of(PAIR, 0, 0), SHARD)
    for way in (BELOW, ABOVE):
        take_in(0, way, 0)
    links.send(("gx end",), gx.at[at, left], from_pair_end, pair)
    step_back(1, 2)
    for way in (BELOW, ABOVE):
        take_in(1, way, 0)

    scale = 1.0 / math.sqrt(16 * 16 * SHARD)
    out_parts = y_sum(0, OUT, chip_sum(OUT, 0, 0))
    in_parts = both_x(0)
    take_pair(0, 0)
    for way in (BELOW, ABOVE):
        take_in(2, way, 0)
    at = pl.ds(row_of(OWN, 0, 0), SHARD)
    gtok_ref[:, right] = gx[at, right]
    links.arrived(("gx end",))
    gtok_ref[:, left] = (gx[at, left].astype(F32) + from_pair_end[...].astype(F32)).astype(BF16)

    links.arrived(("xl", OUT))
    grad_out, in_end = plus(out_parts, read(xl_out, OUT))
    gout_ref[...] = (grad_out * scale).astype(BF16)
    gin_ref[:, cut:] = (in_end * scale).T.astype(BF16)
    (in_start,) = y_sum(2, IN, in_parts)
    gin_ref[:, :cut] = (in_start * scale).T.astype(BF16)

    links.finish()


def hand_over(*refs):
    for src, dst in zip(refs[:3], refs[3:]):
        dst[...] = src[...]


def local(tokens, cotangent, w_in, w_out):
    return layer(tokens, cotangent, w_in, w_out)


def layer(tokens, cotangent, w_in, w_out):
    width, hidden = w_in.shape
    block = width // 16
    group = 16 * SHARD
    mid = 7 * width // 16
    short, long = hidden - 64, hidden + 64
    vmem = pltpu.VMEM
    hbm = pl.BlockSpec(memory_space=pl.ANY)
    return pl.pallas_call(
        kernel,
        out_shape=(
            vmem((SHARD, width), BF16),
            vmem((block, hidden), BF16),
            vmem((hidden, block), BF16),
        ),
        in_specs=[hbm] * 4,
        out_specs=(pl.BlockSpec(memory_space=pltpu.VMEM),) * 3,
        scratch_shapes=[
            vmem((group, width), BF16),
            vmem((group, width), BF16),
            vmem((width, hidden), BF16),
            vmem((hidden, width), BF16),
            vmem((hidden, width), BF16),
            vmem((width, hidden), BF16),
            vmem((CHUNK, hidden), F32),
            vmem((group, hidden), BF16),
            vmem((hidden, group), BF16),
            vmem((hidden, group), BF16),
            vmem((group, width), BF16),
            vmem((2, 2, 4, SHARD, mid), BF16),
            vmem((2, 4, SHARD, width - mid), BF16),
            vmem((8, SHARD, width - mid), BF16),
            vmem((SHARD, mid), BF16),
            vmem((2, Y, short, block), BF16),
            vmem((2, Y, short, block), BF16),
            vmem((2, Y, long, block), BF16),
            vmem((2, Y, long, block), BF16),
            vmem((2, Y, short, block), BF16),
            vmem((2, Y, long, block), BF16),
            vmem((Y, short, block), BF16),
            vmem((long, block), BF16),
            vmem((2, short // 2, block), BF16),
            vmem((2, short, block), BF16),
            vmem((2, 2, long // 2, block), BF16),
            vmem((2, 2, long, block), BF16),
            pltpu.SemaphoreType.DMA((4,)),
            pltpu.SemaphoreType.DMA((MESSAGES,)),
            pltpu.SemaphoreType.DMA((MESSAGES,)),
        ],
        compiler_params=pltpu.CompilerParams(
            collective_id=0, has_side_effects=True, vmem_limit_bytes=VMEM_LIMIT
        ),
        cost_estimate=pl.CostEstimate(
            flops=10 * group * width * hidden,
            bytes_accessed=4 * width * hidden,
            transcendentals=group * hidden,
        ),
    )(tokens, cotangent, w_in, w_out)


def solution(mesh):
    placed = (
        P(("dp", "tensor"), None),
        P(("dp", "tensor"), None),
        P(None, "tensor"),
        P("tensor", None),
    )
    return jax.shard_map(
        local,
        mesh=mesh,
        in_specs=placed,
        out_specs=(P(("dp", "tensor"), None), P("dp", "tensor"), P("tensor", "dp")),
        check_vma=False,
    )
```
